128 devices in a mesh: grp: 8 (over z, core), ctx: 16 (over x, y).
Axes of the slice: x: 4, y: 4, z: 4, core: 2. Of those that a mesh axis runs over, the one named last changes fastest.
Arguments:
- index_query: bfloat16 [256, 8192], P(('grp', 'ctx')), may hold values from -6 to 6
- index_weights: bfloat16 [256, 64], P(('grp', 'ctx')), may hold values from -0.125 to 0.125
- index_keys: bfloat16 [1048576, 128], P(('grp', 'ctx')), may hold values from -6 to 6
- key_scales: float32 [1048576], P(('grp', 'ctx')), may hold values from 0.25 to 4
- attn_query: bfloat16 [256, 128, 576], P(('grp', 'ctx')), may hold values from -360 to 360
- compact_cache: bfloat16 [1048576, 576], P(('grp', 'ctx')), may hold values from -6 to 6
- top_pos: int32 [256, 16, 256], P(('grp', 'ctx')), may hold values from 0 to 8191, as said below
- owner_counts: int32 [256, 16], P(('grp', 'ctx')), may hold values from 1 to 256, 2048 in all within a row
- moe_input: bfloat16 [256, 7168], P(('grp', 'ctx')), may hold values from -6 to 6
- expert_ids: int32 [256, 8], P(('grp', 'ctx')), may hold values from 0 to 15, all different within a row
- expert_gates: float32 [256, 8], P(('grp', 'ctx')), may hold values from 0.05 to 0.5
- gate_proj: bfloat16 [16, 7168, 2048], P('grp', None, 'ctx'), may hold values from -0.0625 to 0.0625
- up_proj: bfloat16 [16, 7168, 2048], P('grp', None, 'ctx'), may hold values from -0.0625 to 0.0625
- down_proj: bfloat16 [16, 2048, 7168], P('grp', 'ctx'), may hold values from -0.125 to 0.125
Outputs:
- index_scores: float32 [256, 131072], P('grp', 'ctx')
- attn_out: bfloat16 [256, 128, 512], P(('grp', 'ctx'))
- moe_out: bfloat16 [256, 7168], P(('grp', 'ctx'))
The draws below stay inside these ranges and needn't reach their ends.
Inputs may be any that keep to these rules, and one draw needn't show every extreme that they name: `top_pos`: for each sample row and device, the first owner_counts slots hold distinct positions; later slots hold arbitrary positions. `owner_counts`: each sample row's counts sum to 2048, and some device holds exactly 256 of them. `expert_ids`: each row names 8 different experts.
All inputs are finite; a program needn't handle non-finite values.
Results may differ from the reference program's by a relative error of at most 0.014.
Values may be sent and summed in bfloat16 or wider, within the bound.
A program may use at most 256 MiB of HBM per device.

```python
import math
import jax
import jax.numpy as jnp
import numpy as np
from jax import lax

D = 7168
ATTENTION_HEADS = 128
LATENT_RANK = 512
ROTARY_WIDTH = 64
IHEADS = 64
IDIM = 128
FF_E = 2048
TOP = 8
TOPK = 2048
ROWS_DEV = 2
CACHE_DEV = 8192
CAP = 256
EXPERTS = 16
SAMPLE_ROWS = 256
PROMPT_POSITIONS = 131072
N_GRP = 8
N_CTX = 16


def draw_attn_query(key, part):
    key = jax.random.fold_in(key, 11)
    value_rows = jnp.clip(jax.random.normal(key, (SAMPLE_ROWS, ATTENTION_HEADS, LATENT_RANK + ROTARY_WIDTH), jnp.float32), -6.0, 6.0)
    return value_rows.astype(jnp.bfloat16)


def pick_positions(subkey):
    return jax.random.permutation(subkey, CACHE_DEV)[:CAP]


def draw_top_pos(key, part):
    key = jax.random.fold_in(key, 23)
    subkeys = jax.random.split(key, SAMPLE_ROWS * N_CTX)
    chosen = jax.vmap(pick_positions)(subkeys)
    return chosen.reshape(SAMPLE_ROWS, N_CTX, CAP).astype(jnp.int32)


def shard_levels(own_key, dims, cuts, least, top_value):
    def one(axis_at, blocks):
        steps = jax.random.uniform(jax.random.fold_in(jax.random.fold_in(own_key, 6), axis_at), (blocks,), jnp.float32, least / len(cuts), top_value / len(cuts))
        return jnp.repeat(jnp.exp(steps), dims[axis_at] // blocks).reshape((-1,) + (1,) * (len(dims) - axis_at - 1))

    loudness = one(*cuts[0])
    for cut in cuts[1:]:
        loudness = loudness * one(*cut)
    return loudness


def distinct(key, rows, number_of, top, lift):
    ranking = jax.random.permutation(jax.random.fold_in(key, 1), number_of)
    favour = ranking
    for power in range(3):
        favour = favour * favour // number_of
    favour = favour * lift // number_of
    lots = jax.random.randint(jax.random.fold_in(key, 2), (rows, number_of), 0, 4096) + favour
    holders = jax.random.permutation(jax.random.fold_in(key, 3), rows)[jnp.arange(number_of) % rows]
    lots = jnp.where(jnp.arange(rows)[:, None] == holders[None, :], 1 << 14, lots)
    score = lots * number_of + jnp.arange(number_of)
    return lax.top_k(score.astype(jnp.int32), top)[1].astype(jnp.int32)


def split_up(number_of, total, most, lean):
    loads = [(1 << 20) // math.isqrt(standing ** lean) + 1 for standing in range(2, number_of + 1)]
    rest, given = total - most - (number_of - 1), [1] * (number_of - 1)
    while rest > 0:
        free = [i for i in range(number_of - 1) if given[i] < most]
        whole, budget = sum([loads[i] for i in free]), rest
        for i in free:
            more = min(most - given[i], max(1, budget * loads[i] // whole), rest)
            given[i] = given[i] + more
            rest = rest - more
    return np.array([most] + given)


def ragged_sizes(rng, count, total, most, lean):
    if count == 2:
        one = jax.random.randint(rng, (), max(1, total - most), min(most, total - 1) + 1)
        return jnp.stack([one, total - one])
    lengths = jnp.asarray(split_up(count, total, most, lean), jnp.int32)
    pairs = (count - 1) // 2
    source_of, taker = lengths[1:1 + 2 * pairs:2], lengths[2:2 + 2 * pairs:2]
    margin = jnp.minimum(source_of - 1, most - taker)
    shifted = jax.random.randint(jax.random.fold_in(rng, 1), (pairs,), 0, 1 << 20) % (margin + 1)
    lengths = lengths.at[1:1 + 2 * pairs:2].set(source_of - shifted).at[2:2 + 2 * pairs:2].set(taker + shifted)
    return lengths[jax.random.permutation(jax.random.fold_in(rng, 2), count)]


def normal_values(stream_key, extent, deviation, limit, cuts=(), held_as=jnp.bfloat16):
    gain = shard_levels(stream_key, extent, cuts, -0.22, 0.18) if cuts else 1.0
    array = jax.random.normal(stream_key, extent, jnp.float32) * deviation * gain
    return jnp.minimum(jnp.maximum(array, -limit), limit).astype(held_as)


def setup_inputs(seed: int = 0) -> dict:
    key_list = jax.random.split(jax.random.key(seed), 15)
    index_query = normal_values(key_list[0], (SAMPLE_ROWS, IHEADS * IDIM), 1.0, 6.0, ((0, 128),))
    index_weights = normal_values(key_list[1], (SAMPLE_ROWS, IHEADS), 0.02, 0.125, ((0, 128),))
    index_keys = normal_values(key_list[2], (N_GRP * PROMPT_POSITIONS, IDIM), 1.0, 6.0, ((0, 128),))
    key_scales = jnp.clip(jnp.exp(math.log(4.0) - 2.7725887 * jax.random.uniform(key_list[3], (N_GRP * PROMPT_POSITIONS,), jnp.float32) ** shard_levels(key_list[3], (N_GRP * PROMPT_POSITIONS,), ((0, 128),), -0.2, 0.2)), 0.25, 4.0)
    attn_query = draw_attn_query(jax.random.fold_in(key_list[14], 71), 0)
    compact_cache = normal_values(key_list[5], (N_GRP * PROMPT_POSITIONS, LATENT_RANK + ROTARY_WIDTH), 1.0, 6.0, ((0, 128),))
    top_pos = draw_top_pos(jax.random.fold_in(key_list[14], 71), 0)
    owner_counts = jax.vmap(lambda own: ragged_sizes(own, N_CTX, TOPK, CAP, 2))(jax.random.split(key_list[7], SAMPLE_ROWS)).reshape((SAMPLE_ROWS, N_CTX)).astype(jnp.int32)
    moe_input = normal_values(key_list[8], (SAMPLE_ROWS, D), 1.0, 6.0, ((0, 128),))
    expert_ids = distinct(key_list[9], SAMPLE_ROWS, EXPERTS, TOP, 8192)
    expert_gates = jnp.clip(jnp.exp(math.log(0.5) - 2.3025851 * jax.random.uniform(key_list[10], (SAMPLE_ROWS, TOP), jnp.float32) ** shard_levels(key_list[10], (SAMPLE_ROWS, TOP), ((0, 128),), -0.2, 0.2)), 0.05, 0.5)
    gate_proj = normal_values(key_list[11], (EXPERTS, D, FF_E), D ** -0.5, 0.0625, ((0, 8), (2, 16)))
    up_proj = normal_values(key_list[12], (EXPERTS, D, FF_E), D ** -0.5, 0.0625, ((0, 8), (2, 16)))
    down_proj = normal_values(key_list[13], (EXPERTS, FF_E, D), FF_E ** -0.5, 0.125, ((0, 8), (1, 16)))
    return {"index_query": index_query, "index_weights": index_weights, "index_keys": index_keys, "key_scales": key_scales, "attn_query": attn_query, "compact_cache": compact_cache, "top_pos": top_pos, "owner_counts": owner_counts, "moe_input": moe_input, "expert_ids": expert_ids, "expert_gates": expert_gates, "gate_proj": gate_proj, "up_proj": up_proj, "down_proj": down_proj}


score_scale = 192.0 ** -0.5


def reference(index_query, index_weights, index_keys, key_scales, attn_query, compact_cache, top_pos, owner_counts, moe_input, expert_ids, expert_gates, gate_proj, up_proj, down_proj):
    group_rows = ROWS_DEV * N_CTX
    context = N_CTX * CACHE_DEV
    queries = index_query.reshape(N_GRP, group_rows * IHEADS, IDIM)
    head_weights = index_weights.astype(jnp.float32).reshape(N_GRP, group_rows, IHEADS)
    keys_all = index_keys.reshape(N_GRP, N_CTX, CACHE_DEV, IDIM)
    scales_all = key_scales.reshape(N_GRP, N_CTX, CACHE_DEV)

    def per_group(inputs):
        query_rows, weight_rows, key_rows, scale_rows = inputs

        def per_owner(paired):
            owner_keys, owner_scale = paired
            products = jnp.dot(query_rows, owner_keys.T, preferred_element_type=jnp.float32)
            active = jnp.maximum(products, 0.0).reshape(group_rows, IHEADS, CACHE_DEV)
            return jnp.einsum("rhs,rh->rs", active, weight_rows) * owner_scale[None, :]

        return lax.map(per_owner, (key_rows, scale_rows))

    blocks = lax.map(per_group, (queries, head_weights, keys_all, scales_all))
    index_scores = blocks.transpose(0, 2, 1, 3).reshape(N_GRP * group_rows, context)

    owner_base = jnp.arange(N_CTX, dtype=jnp.int32) * CACHE_DEV
    slot_index = jnp.arange(CAP, dtype=jnp.int32)

    def attend_row(inputs):
        query, positions, counts, row_id = inputs
        group_id = row_id // group_rows
        global_rows = (group_id * context + owner_base[:, None] + positions).reshape(-1).astype(jnp.int32)
        collected_rows = jnp.take(compact_cache, global_rows, axis=0)
        live_slot = (slot_index[None, :] < counts[:, None]).reshape(-1)
        scores = jnp.dot(query, collected_rows.T, preferred_element_type=jnp.float32) * score_scale
        row_peak = jnp.max(jnp.where(live_slot[None, :], scores, -1e30), axis=1, keepdims=True)
        exponent = jnp.where(live_slot[None, :], jnp.exp(scores - row_peak), 0.0)
        denominator = jnp.sum(exponent, axis=1)
        softmax_weights = exponent.astype(jnp.bfloat16)
        weighted_total = jnp.dot(softmax_weights, collected_rows[:, :LATENT_RANK], preferred_element_type=jnp.float32)
        return (weighted_total / denominator[:, None]).astype(jnp.bfloat16)

    attn_out = lax.map(attend_row, (attn_query, top_pos, owner_counts, jnp.arange(SAMPLE_ROWS, dtype=jnp.int32)))

    expert_range = jnp.arange(EXPERTS, dtype=jnp.int32)
    gate_table = jnp.sum(expert_gates[:, :, None] * (expert_ids[:, :, None] == expert_range[None, None, :]).astype(jnp.float32), axis=1)
    mixed = jnp.zeros((SAMPLE_ROWS, D), jnp.float32)
    for expert in range(EXPERTS):
        gate_part = jnp.dot(moe_input, gate_proj[expert], preferred_element_type=jnp.float32)
        up_part = jnp.dot(moe_input, up_proj[expert], preferred_element_type=jnp.float32)
        hidden = (jax.nn.silu(gate_part) * up_part).astype(jnp.bfloat16)
        output = jnp.dot(hidden, down_proj[expert], preferred_element_type=jnp.float32)
        mixed = mixed + gate_table[:, expert, None] * output
    return index_scores, attn_out, mixed.astype(jnp.bfloat16)
```

```python
import jax
import jax.numpy as jnp
from jax import lax
from jax.experimental import pallas as pl
from jax.experimental.pallas import tpu as pltpu
from jax.sharding import PartitionSpec as P

MESH = pl.DeviceIdType.MESH
BF16, F32 = jnp.bfloat16, jnp.float32
HEADS, LATENT, WIDTH = 128, 512, 576
IHEADS, IDIM = 64, 128
CACHE, CAP = 8192, 256
MODEL = 7168
CHUNKS = MODEL // 128
TOKW = MODEL + 128
HALF = 288
KEYB = 512
SCALE = 192.0**-0.5
ANY, VMEM, SMEM = pl.ANY, pltpu.VMEM, pltpu.SMEM


class Place:
    def __init__(self):
        self.g, self.c = lax.axis_index("grp"), lax.axis_index("ctx")
        self.z, self.core = self.g // 2, lax.rem(self.g, 2)
        self.x, self.y = self.c // 4, lax.rem(self.c, 4)

    def ctx(self, axis, d, e=0):
        dx, dy = (d, e) if axis == 0 else (e, d)
        return lax.rem(self.x + dx + 4, 4) * 4 + lax.rem(self.y + dy + 4, 4)

    def near(self, axis, d):
        return (self.g, self.ctx(axis, d))

    def peer(self, k):
        return (self.g, lax.rem(self.c + k, 16))

    def grp(self, d, other=False):
        core = 1 - self.core if other else self.core
        return lax.rem(self.z + d + 4, 4) * 2 + core

    def greet(self):
        bar = pltpu.get_barrier_semaphore()
        friends = [self.peer(k) for k in range(1, 16)]
        friends += [(self.grp(1), self.c), (self.grp(-1), self.c), (self.grp(0, True), self.c)]
        for f in friends:
            pl.semaphore_signal(bar, inc=1, device_id=f, device_id_type=MESH)
        pl.semaphore_wait(bar, len(friends))


class Post:
    def __init__(self, send_sems, recv_sems):
        self.ss, self.rs, self.out = send_sems, recv_sems, []

    def send(self, src, dst, dev):
        i = len(self.out)
        cp = pltpu.make_async_remote_copy(
            src_ref=src, dst_ref=dst, send_sem=self.ss.at[i], recv_sem=self.rs.at[i], device_id=dev, device_id_type=MESH
        )
        cp.start()
        self.out.append(cp)
        return cp

    def finish(self):
        for cp in self.out:
            cp.wait_send()


def plane_gather(post, at, part):
    def both(ref, axis):
        return post.send(ref, ref, at.near(axis, 1)), post.send(ref, ref, at.near(axis, -1))

    def split(src, h, axis, plus, minus):
        plus.wait_recv()
        lo = part(src(-1), h, 0)
        a = post.send(lo, lo, at.near(axis, 1))
        minus.wait_recv()
        hi = part(src(1), h, 1)
        return a, post.send(hi, hi, at.near(axis, -1))

    first = [both(part(at.c, h, None), h) for h in (0, 1)]
    across = {(h, 0): both(part(at.c, h, None), 1 - h) for h in (0, 1)}
    yield
    second = []
    for h in (0, 1):
        second.append(split(lambda d: at.ctx(h, d), h, h, *first[h]))
        for d in (-1, 1):
            across[h, d] = both(part(at.ctx(h, d), h, None), 1 - h)
    yield
    for h in (0, 1):
        for cp in second[h]:
            cp.wait_recv()
        across[h, 2] = both(part(at.ctx(h, 2), h, None), 1 - h)
    last = []
    for d in (0, -1, 1, 2):
        yield
        for h in (0, 1):
            last += split(lambda e: at.ctx(h, d, e), h, 1 - h, *across[h, d])
    yield
    for cp in last:
        cp.wait_recv()


def gather_kernel(
    small, pos, aq, keys, kscale,
    qall, pall, xall, scores,
    agbuf, keybuf, wb, xf, xown, lsem, ss, rs, kss, krs, zss, zrs,
):
    at = Place()
    at.greet()
    own_small = pltpu.make_async_copy(small, agbuf.at[at.c], lsem.at[0])
    own_q = pltpu.make_async_copy(aq, qall.at[at.c], lsem.at[1])
    own_pos = pltpu.make_async_copy(pos.at[at.c], pall.at[at.c], lsem.at[2])
    load_keys = pltpu.make_async_copy(keys, keybuf, lsem.at[3])
    for cp in (own_small, own_q, own_pos, load_keys):
        cp.start()
    own_small.wait()
    few = Post(kss, krs)
    quick = plane_gather(few, at, lambda i, h, q: agbuf.at[i, h] if q is None else agbuf.at[i, h, pl.ds(64 * q, 64)])
    next(quick)
    places = [few.send(pos.at[at.peer(k)[1]], pall.at[at.c], at.peer(k)) for k in range(1, 16)]
    own_q.wait()
    many = Post(ss, rs)
    big = plane_gather(
        many, at, lambda i, h, q: qall.at[i, h] if q is None else qall.at[i, h, pl.ds(HALF * q, HALF)]
    )
    next(big)
    for _ in quick:
        pass
    next(big)

    def widen(i, _):
        xf[pl.ds(pl.multiple_of(i * 128, 128), 64), :] = agbuf[i, 0, 64:128, :].astype(F32)
        xf[pl.ds(pl.multiple_of(i * 128 + 64, 64), 64), :] = agbuf[i, 1, 64:128, :].astype(F32)
        wide = [jnp.broadcast_to(xf[pl.ds(i * 128 + 64 * t + 57, 1), :], (128, 128)).T[0:64, :] for t in (0, 1)]
        wb[i] = jnp.concatenate(wide, axis=0)
        return 0

    lax.fori_loop(0, 16, widen, 0)

    def lay(k, _):
        xown[:, pl.ds(pl.multiple_of(k * 128, 128), 128)] = xf[pl.ds(k, 32, stride=64), :].astype(BF16)
        return 0

    lax.fori_loop(0, CHUNKS + 1, lay, 0)
    zpost = Post(zss, zrs)
    up, down, over = (at.grp(1), at.c), (at.grp(-1), at.c), (at.grp(0, True), at.c)
    own_x = pltpu.make_async_copy(xown, xall.at[at.g], lsem.at[4])
    own_x.start()
    z_up = zpost.send(xown, xall.at[at.g], up)
    z_down = zpost.send(xown, xall.at[at.g], down)
    z_over = [zpost.send(xown, xall.at[at.g], over)]

    load_keys.wait()

    def index_block(b, _):
        cols = pl.ds(pl.multiple_of(b * KEYB, KEYB), KEYB)
        k = keybuf[cols, :]

        def four(i, _):
            q = jnp.concatenate([agbuf[4 * i + u, t, 0:64, :] for u in range(4) for t in range(2)], axis=0)
            p = lax.dot_general(q, k, (((1,), (1,)), ((), ())), preferred_element_type=F32)
            rows = []
            for u in range(4):
                w = jnp.concatenate([wb[4 * i + u]] * (KEYB // 128), axis=1)
                a = jnp.maximum(p[u * 128 : (u + 1) * 128], 0.0) * w
                rows += [jnp.sum(a[t * 64 : (t + 1) * 64], axis=0, keepdims=True) for t in (0, 1)]
            s = jnp.concatenate(rows, axis=0) * kscale[:, cols]
            scores[pl.ds(pl.multiple_of(i * 8, 8), 8), cols] = s
            return 0

        lax.fori_loop(0, 4, four, 0)
        return 0

    blocks = CACHE // KEYB
    lax.fori_loop(0, blocks // 4, index_block, 0)
    next(big)
    lax.fori_loop(blocks // 4, blocks // 2, index_block, 0)
    next(big)
    z_up.wait_recv()
    low = xall.at[at.grp(-1)]
    z_low = zpost.send(low.at[pl.ds(0, 16)], low.at[pl.ds(0, 16)], up)
    z_over.append(zpost.send(low, low, over))
    z_down.wait_recv()
    high = xall.at[at.grp(1)]
    z_high = zpost.send(high.at[pl.ds(16, 16)], high.at[pl.ds(16, 16)], down)
    z_over.append(zpost.send(high, high, over))
    lax.fori_loop(blocks // 2, 3 * blocks // 4, index_block, 0)
    next(big)
    lax.fori_loop(3 * blocks // 4, blocks, index_block, 0)
    next(big)
    z_low.wait_recv()
    z_high.wait_recv()
    far = xall.at[at.grp(2)]
    z_over.append(zpost.send(far, far, over))
    for _ in big:
        pass
    for cp in z_over + places:
        cp.wait_recv()
    own_pos.wait()
    own_x.wait()
    for post in (few, many, zpost):
        post.finish()


def gather_all(small, pos, aq, keys, kscale):
    dma = pltpu.SemaphoreType.DMA
    return pl.pallas_call(
        gather_kernel,
        out_shape=(
            jax.ShapeDtypeStruct((16, 2, WIDTH, HEADS), BF16),
            jax.ShapeDtypeStruct((16, 8, 128), jnp.int32),
            jax.ShapeDtypeStruct((8, 32, TOKW), BF16),
            jax.ShapeDtypeStruct((32, CACHE), F32),
        ),
        in_specs=[pl.BlockSpec(memory_space=ANY)] * 4 + [pl.BlockSpec(memory_space=VMEM)],
        out_specs=(pl.BlockSpec(memory_space=ANY),) * 3 + (pl.BlockSpec(memory_space=VMEM),),
        scratch_shapes=[
            VMEM((16, 2, 128, 128), BF16),
            VMEM((CACHE, IDIM), BF16),
            VMEM((16, 128, 128), F32),
            VMEM((2048, 128), F32),
            VMEM((32, TOKW), BF16),
            dma((5,)),
            dma((40,)),
            dma((40,)),
            dma((55,)),
            dma((55,)),
            dma((8,)),
            dma((8,)),
        ],
        compiler_params=pltpu.CompilerParams(collective_id=0, has_side_effects=True, vmem_limit_bytes=48 * 2**20),
    )(small, pos, aq, keys, kscale)


def attend_kernel(pos, cache, q, o_ref, l_ref, cbuf, rows, dst, kbf, qbuf, csem, qsem):
    loads = []
    for i in range(8):
        cols = pl.ds(1024 * i, 1024)
        loads.append(pltpu.make_async_copy(cache.at[:, cols], cbuf.at[:, cols], csem.at[i]))
        loads[-1].start()
    load_q = pltpu.make_async_copy(q, qbuf, qsem)
    load_q.start()
    eye = (
        lax.broadcasted_iota(jnp.int32, (256, 256), 0) == lax.broadcasted_iota(jnp.int32, (256, 256), 1)
    ).astype(BF16)
    dst[...] = jnp.zeros_like(dst)
    for i in range(8):
        loads[i].wait()

        def turn(b, _):
            off = pl.multiple_of(i * 1024 + b * 256, 256)
            t = lax.dot_general(
                eye, cbuf[:, pl.ds(off, 256)], (((1,), (1,)), ((), ())), preferred_element_type=F32
            )
            for c in range(5):
                w = min(128, WIDTH - 128 * c)
                rows[pl.ds(off * 8 + c, 256, stride=8), 0:w] = t[:, c * 128 : c * 128 + w]
            return 0

        lax.fori_loop(0, 4, turn, 0)
    load_q.wait()

    def one(t, _):
        c, h = t // 2, lax.rem(t, 2)
        n = pos[c, 4, h]

        def pick(j, _):
            line, col = 2 * h + j // 8, lax.rem(j, 8) * 16
            for u in range(16):
                s = j * 16 + u
                p = pos[c, line, col + u]
                dst[pl.ds(pl.multiple_of(s * 8, 8), 8), :] = rows[pl.ds(pl.multiple_of(p * 8, 8), 8), :]
            return 0

        lax.fori_loop(0, (n + 15) // 16, pick, 0)
        for i in range(5):
            w = min(128, WIDTH - 128 * i)
            kbf[:, i * 128 : i * 128 + w] = dst[pl.ds(i, CAP, stride=8), 0:w].astype(BF16)
        s = jnp.dot(kbf[...], qbuf[c, h], preferred_element_type=F32) * SCALE
        live = lax.broadcasted_iota(jnp.int32, (CAP, HEADS), 0) < n
        s = jnp.where(live, s, -1e30)
        m = jnp.max(s, axis=0, keepdims=True)
        e = jnp.where(live, jnp.exp(s - m), 0.0)
        l = jnp.sum(e, axis=0, keepdims=True)
        p = (e * (1.0 / l)).T.astype(BF16)
        o_ref[c, h] = jnp.dot(p, kbf[:, 0:LATENT], preferred_element_type=F32).astype(BF16)
        l_ref[c, h] = jnp.broadcast_to(m + jnp.log(l), (8, HEADS))
        return 0

    lax.fori_loop(0, 32, one, 0)


def attend(pos, cache, q):
    return pl.pallas_call(
        attend_kernel,
        out_shape=(
            jax.ShapeDtypeStruct((16, 2, HEADS, LATENT), BF16),
            jax.ShapeDtypeStruct((16, 2, 8, HEADS), F32),
        ),
        in_specs=[pl.BlockSpec(memory_space=SMEM)] + [pl.BlockSpec(memory_space=ANY)] * 2,
        out_specs=(pl.BlockSpec(memory_space=VMEM),) * 2,
        scratch_shapes=[
            VMEM((WIDTH, CACHE), BF16),
            VMEM((CACHE * 8, 128), F32),
            VMEM((CAP * 8, 128), F32),
            VMEM((CAP, WIDTH), BF16),
            VMEM((16, 2, WIDTH, HEADS), BF16),
            pltpu.SemaphoreType.DMA((8,)),
            pltpu.SemaphoreType.DMA,
        ],
        compiler_params=pltpu.CompilerParams(vmem_limit_bytes=58 * 2**20),
    )(pos, cache, q)


def merge(parts, lo, n):
    top = parts[0][1]
    for _, l in parts[1:]:
        top = jnp.maximum(top, l)
    es = [jnp.exp(l - top) for _, l in parts]
    tot = es[0]
    for e in es[1:]:
        tot = tot + e
    inv = 1.0 / tot
    diag = lax.broadcasted_iota(jnp.int32, (n, HEADS), 0) + lo == lax.broadcasted_iota(jnp.int32, (n, HEADS), 1)
    out = None
    for (o, _), e in zip(parts, es):
        w = jnp.broadcast_to((e * inv)[0:1], (n, HEADS))
        col = jnp.sum(jnp.where(diag, w, 0.0), axis=1, keepdims=True)
        term = o.astype(F32) * col
        out = term if out is None else out + term
    return out.astype(BF16), top + jnp.log(tot)


def plane_scatter(post, at, o, l, bufs, result):
    r1, l1, m1, ml1, r2, l2, p1, pl1, r3, l3, m2, ml2, r4, l4 = bufs

    def both(src, lsrc, dst, ldst, dev):
        return post.send(src, dst, dev), post.send(lsrc, ldst, dev)

    def arrive(pair):
        for cp in pair:
            cp.wait_recv()

    s1, s2 = {}, {}
    for h in (0, 1):
        a = 1 - h
        for e in range(4):
            i = at.ctx(a, 2, e)
            s1[h, e] = both(o.at[i, h], l.at[i, h], r1.at[h, e], l1.at[h, e], at.near(a, 1 if e < 2 else -1))
    for h in (0, 1):
        a = 1 - h
        for e in range(4):
            d = 0 if e >= 2 else 1
            i = at.ctx(a, 1 - 2 * d, e)
            s2[h, d, e] = both(o.at[i, h], l.at[i, h], r2.at[h, d, e], l2.at[h, d, e], at.near(a, 1 - 2 * d))
    yield
    for e in (0, 2, 1, 3):
        for h in (0, 1):
            a = 1 - h
            d = 0 if e < 2 else 1
            i = at.ctx(a, 1 - 2 * d, e)
            arrive(s1[h, e])
            m1[h, e], ml1[h, e] = merge([(o[i, h], l[i, h]), (r1[h, e], l1[h, e])], 0, HEADS)
            s2[h, d, e] = both(m1.at[h, e], ml1.at[h, e], r2.at[h, d, e], l2.at[h, d, e], at.near(a, 1 - 2 * d))
        if e == 2:
            yield
    yield
    s3, s4 = {}, {}
    for e in (2, 1, 3, 0):
        for h in (0, 1):
            a = 1 - h
            i = at.ctx(a, 0, e)
            arrive(s2[h, 0, e])
            arrive(s2[h, 1, e])
            p1[h, e], pl1[h, e] = merge(
                [(o[i, h], l[i, h]), (r2[h, 0, e], l2[h, 0, e]), (r2[h, 1, e], l2[h, 1, e])], 0, HEADS
            )
            if e == 2:
                for d in (0, 1):
                    s3[h, d] = both(
                        p1.at[h, 2, pl.ds(64 * d, 64)], pl1.at[h, 2], r3.at[h, d], l3.at[h, d], at.near(h, 1 - 2 * d)
                    )
        yield
    for h in (0, 1):
        for d in (0, 1):
            e = 1 if d == 0 else 3
            arrive(s3[h, d])
            mine = slice(64 * d, 64 * d + 64)
            rest = slice(64 - 64 * d, 128 - 64 * d)
            m2[h, d, rest] = p1[h, e, rest]
            m2[h, d, mine], lm = merge([(p1[h, e, mine], pl1[h, e]), (r3[h, d], l3[h, d])], 64 * d, 64)
            lane = lax.broadcasted_iota(jnp.int32, (8, HEADS), 1)
            ml2[h, d] = jnp.where((lane < 64) if d == 0 else (lane >= 64), lm, pl1[h, e])
            s4[h, d] = both(m2.at[h, d], ml2.at[h, d], r4.at[h, d], l4.at[h, d], at.near(h, 1 - 2 * d))
    yield
    for h in (0, 1):
        arrive(s4[h, 0])
        arrive(s4[h, 1])
        result[h], _ = merge([(p1[h, 0], pl1[h, 0]), (r4[h, 0], l4[h, 0]), (r4[h, 1], l4[h, 1])], 0, HEADS)


def reduce_kernel(
    o, l, xall, gate, up, dn,
    attn, moe,
    xbuf, wgu, dnbuf, acc, hid, mp, rc, rz1, rz2, yf, yb, ry,
    r1, l1, m1, ml1, r2, l2, p1, pl1, r3, l3, m2, ml2, r4, l4,
    lsem, ss, rs, zss, zrs,
):
    at = Place()
    loads = [pltpu.make_async_copy(xall, xbuf, lsem.at[0])]
    for e in (0, 1):
        loads.append(pltpu.make_async_copy(gate.at[e], wgu.at[e, :, pl.ds(0, 128)], lsem.at[1 + e]))
        loads.append(pltpu.make_async_copy(up.at[e], wgu.at[e, :, pl.ds(128, 128)], lsem.at[3 + e]))
    load_dn = pltpu.make_async_copy(dn, dnbuf, lsem.at[5])
    for cp in loads + [load_dn]:
        cp.start()
    at.greet()
    post = Post(ss, rs)
    flow = plane_scatter(post, at, o, l, (r1, l1, m1, ml1, r2, l2, p1, pl1, r3, l3, m2, ml2, r4, l4), attn)
    next(flow)

    for cp in loads:
        cp.wait()
    acc[...] = jnp.zeros_like(acc)

    def expand(k, _):
        cols = pl.ds(pl.multiple_of(k * 1024, 1024), 1024)
        x = xbuf[:, :, cols].reshape(256, 1024)
        for e in (0, 1):
            acc[e] += jnp.dot(x, wgu[e, cols, :], preferred_element_type=F32)
        return 0

    lax.fori_loop(0, MODEL // 1024, expand, 0)
    gates = xbuf[:, :, MODEL:TOKW].reshape(256, 128).astype(F32)
    lane = lax.broadcasted_iota(jnp.int32, (256, 128), 1)
    for e in (0, 1):
        own = at.g * 2 + e
        col = jnp.sum(jnp.where((lane == own) | (lane == own + 16), gates, 0.0), axis=1, keepdims=True)
        gp, upart = acc[e, :, 0:128], acc[e, :, 128:256]
        hid[:, e * 128 : e * 128 + 128] = (gp / (1.0 + jnp.exp(-gp)) * upart * col).astype(BF16)
    load_dn.wait()

    def contract(k, _):
        cols = pl.ds(pl.multiple_of(k * 1024, 1024), 1024)
        mp[:, :, cols] = jnp.dot(hid[...], dnbuf[:, cols], preferred_element_type=F32).astype(BF16).reshape(8, 32, 1024)
        return 0

    lax.fori_loop(0, MODEL // 1024, contract, 0)
    zpost = Post(zss, zrs)
    zup, zdown, over = (at.grp(1), at.c), (at.grp(-1), at.c), (at.grp(0, True), at.c)
    order = (2, 1, -1, 0)
    swaps = [zpost.send(mp.at[at.grp(d, True)], rc.at[i], over) for i, d in enumerate(order)]
    next(flow)
    next(flow)

    def add(i, d):
        swaps[i].wait_recv()
        b = at.grp(d)
        mp[b] = (mp[b].astype(F32) + rc[i].astype(F32)).astype(BF16)

    add(0, 2)
    far = mp.at[at.grp(2)]
    za = zpost.send(far.at[pl.ds(0, 16)], rz1.at[0], zup)
    zb = zpost.send(far.at[pl.ds(16, 16)], rz1.at[1], zdown)
    next(flow)
    add(1, 1)
    add(2, -1)
    next(flow)
    za.wait_recv()
    b = at.grp(1)
    mp[b, 0:16] = (mp[b, 0:16].astype(F32) + rz1[0].astype(F32)).astype(BF16)
    zc = zpost.send(mp.at[b], rz2.at[0], zup)
    zb.wait_recv()
    b2 = at.grp(-1)
    mp[b2, 16:32] = (mp[b2, 16:32].astype(F32) + rz1[1].astype(F32)).astype(BF16)
    zd = zpost.send(mp.at[b2], rz2.at[1], zdown)
    swaps[3].wait_recv()
    next(flow)
    next(flow)
    zc.wait_recv()
    zd.wait_recv()

    def spread(k, _):
        cols = pl.ds(pl.multiple_of(k * 128, 128), 128)
        t = mp[at.g, :, cols].astype(F32) + rc[3, :, cols].astype(F32)
        t = t + rz2[0, :, cols].astype(F32) + rz2[1, :, cols].astype(F32)
        yf[pl.ds(k, 32, stride=CHUNKS), :] = t
        return 0

    lax.fori_loop(0, CHUNKS, spread, 0)

    def narrow(i, _):
        yb[i] = yf[pl.ds(pl.multiple_of(i * 112, 8), 112), :].astype(BF16)
        return 0

    lax.fori_loop(0, 16, narrow, 0)
    home = [zpost.send(yb.at[at.peer(k)[1]], ry.at[k - 1], at.peer(k)) for k in range(1, 16)]
    for _ in flow:
        pass
    total = yb[at.c].astype(F32)
    for k, cp in enumerate(home):
        cp.wait_recv()
        total = total + ry[k].astype(F32)
    moe[...] = total.astype(BF16)
    post.finish()
    zpost.finish()


def reduce_all(o, l, xall, gate, up, dn):
    dma = pltpu.SemaphoreType.DMA
    ob, lb = (HEADS, LATENT), (8, HEADS)

    def pair(*lead, block=ob):
        return [VMEM(lead + block, BF16), VMEM(lead + lb, F32)]

    return pl.pallas_call(
        reduce_kernel,
        out_shape=(jax.ShapeDtypeStruct((2, HEADS, LATENT), BF16), jax.ShapeDtypeStruct((112, 128), BF16)),
        in_specs=[pl.BlockSpec(memory_space=VMEM)] * 2 + [pl.BlockSpec(memory_space=ANY)] * 4,
        out_specs=(pl.BlockSpec(memory_space=VMEM),) * 2,
        scratch_shapes=[
            VMEM((8, 32, TOKW), BF16),
            VMEM((2, MODEL, 256), BF16),
            VMEM((256, MODEL), BF16),
            VMEM((2, 256, 256), F32),
            VMEM((256, 256), BF16),
            VMEM((8, 32, MODEL), BF16),
            VMEM((4, 32, MODEL), BF16),
            VMEM((2, 16, MODEL), BF16),
            VMEM((2, 32, MODEL), BF16),
            VMEM((32 * CHUNKS, 128), F32),
            VMEM((16, 112, 128), BF16),
            VMEM((15, 112, 128), BF16),
            *pair(2, 4),
            *pair(2, 4),
            *pair(2, 2, 4),
            *pair(2, 4),
            *pair(2, 2, block=(64, LATENT)),
            *pair(2, 2),
            *pair(2, 2),
            dma((6,)),
            dma((64,)),
            dma((64,)),
            dma((23,)),
            dma((23,)),
        ],
        compiler_params=pltpu.CompilerParams(collective_id=1, has_side_effects=True, vmem_limit_bytes=58 * 2**20),
    )(o, l, xall, gate, up, dn)


def local(
    index_query, index_weights, index_keys, key_scales, attn_query, compact_cache, top_pos, owner_counts,
    moe_input, expert_ids, expert_gates, gate_proj, up_proj, down_proj,
):
    experts = lax.axis_size("grp") * gate_proj.shape[0]
    matches = expert_ids[:, :, None] == jnp.arange(experts, dtype=jnp.int32)[None, None, :]
    table = jnp.sum(expert_gates[:, :, None] * matches.astype(F32), axis=1)
    high = lax.reduce_precision(table, 8, 7)
    gates = jnp.concatenate([high, table - high, jnp.zeros((2, 96), F32)], axis=1).astype(BF16)
    weights = jnp.pad(index_weights, ((0, 0), (0, 64)))
    small = jnp.concatenate(
        [
            index_query.reshape(2, IHEADS, IDIM),
            moe_input.reshape(2, CHUNKS, 128),
            gates[:, None],
            weights[:, None],
            jnp.zeros((2, 6, 128), BF16),
        ],
        axis=1,
    )
    places = jnp.transpose(top_pos, (1, 0, 2)).reshape(16, 4, 128)
    counts = jnp.pad(owner_counts.T.reshape(16, 1, 2), ((0, 0), (0, 3), (0, 126)))
    pos = jnp.concatenate([places, counts], axis=1)
    qall, pall, xall, index_scores = gather_all(
        small, pos, jnp.swapaxes(attn_query, 1, 2), index_keys, key_scales.reshape(1, CACHE)
    )
    o, l = attend(pall, compact_cache.T, qall)
    attn_out, moe_out = reduce_all(o, l, xall, gate_proj, up_proj, down_proj.reshape(256, MODEL))
    return index_scores, attn_out, moe_out.reshape(2, MODEL)


def solution(mesh):
    one = P(("grp", "ctx"))
    in_specs = (one,) * 11 + (P("grp", None, "ctx"), P("grp", None, "ctx"), P("grp", "ctx", None))
    return jax.shard_map(
        local, mesh=mesh, in_specs=in_specs, out_specs=(P("grp", "ctx"), one, one), check_vma=False
    )
```

```python
import jax
import jax.numpy as jnp
from jax import lax
from jax.experimental import pallas as pl
from jax.experimental.pallas import tpu as pltpu
from jax.sharding import PartitionSpec as P

MESH = pl.DeviceIdType.MESH
BF16, F32 = jnp.bfloat16, jnp.float32
HEADS, LATENT, WIDTH = 128, 512, 576
IHEADS, IDIM = 64, 128
CACHE, CAP = 8192, 256
MODEL = 7168
CHUNKS = MODEL // 128
TOKW = MODEL + 128
HALF = 288
KEYB = 2048
PITCH = 5
SCALE = 192.0**-0.5
ANY, VMEM, SMEM = pl.ANY, pltpu.VMEM, pltpu.SMEM


class Place:
    def __init__(self):
        self.g, self.c = lax.axis_index("grp"), lax.axis_index("ctx")
        self.z, self.core = self.g // 2, lax.rem(self.g, 2)
        self.x, self.y = self.c // 4, lax.rem(self.c, 4)

    def ctx(self, axis, d, e=0):
        dx, dy = (d, e) if axis == 0 else (e, d)
        return lax.rem(self.x + dx + 4, 4) * 4 + lax.rem(self.y + dy + 4, 4)

    def near(self, axis, d):
        return (self.g, self.ctx(axis, d))

    def peer(self, k):
        return (self.g, lax.rem(self.c + k, 16))

    def grp(self, d, other=False):
        core = 1 - self.core if other else self.core
        return lax.rem(self.z + d + 4, 4) * 2 + core

    def greet(self):
        bar = pltpu.get_barrier_semaphore()
        friends = [self.peer(k) for k in range(1, 16)]
        friends += [(self.grp(1), self.c), (self.grp(-1), self.c), (self.grp(0, True), self.c)]
        for f in friends:
            pl.semaphore_signal(bar, inc=1, device_id=f, device_id_type=MESH)
        pl.semaphore_wait(bar, len(friends))


class Post:
    def __init__(self, send_sems, recv_sems):
        self.ss, self.rs, self.out = send_sems, recv_sems, []

    def send(self, src, dst, dev):
        i = len(self.out)
        cp = pltpu.make_async_remote_copy(
            src_ref=src, dst_ref=dst, send_sem=self.ss.at[i], recv_sem=self.rs.at[i], device_id=dev, device_id_type=MESH
        )
        cp.start()
        self.out.append(cp)
        return cp

    def finish(self):
        for cp in self.out:
            cp.wait_send()


def plane_gather(post, at, part):
    def both(ref, axis):
        return post.send(ref, ref, at.near(axis, 1)), post.send(ref, ref, at.near(axis, -1))

    def split(src, h, axis, plus, minus):
        plus.wait_recv()
        lo = part(src(-1), h, 0)
        a = post.send(lo, lo, at.near(axis, 1))
        minus.wait_recv()
        hi = part(src(1), h, 1)
        return a, post.send(hi, hi, at.near(axis, -1))

    first = [both(part(at.c, h, None), h) for h in (0, 1)]
    across = {(h, 0): both(part(at.c, h, None), 1 - h) for h in (0, 1)}
    yield
    second = []
    for h in (0, 1):
        second.append(split(lambda d: at.ctx(h, d), h, h, *first[h]))
        for d in (-1, 1):
            across[h, d] = both(part(at.ctx(h, d), h, None), 1 - h)
    yield
    for h in (0, 1):
        for cp in second[h]:
            cp.wait_recv()
        across[h, 2] = both(part(at.ctx(h, 2), h, None), 1 - h)
    last = []
    for d in (0, -1, 1, 2):
        yield
        for h in (0, 1):
            last += split(lambda e: at.ctx(h, d, e), h, 1 - h, *across[h, d])
    yield
    for cp in last:
        cp.wait_recv()


def gather_kernel(
    iq, iw, tok, ids, eg, tp, oc, kscale, aq, keys, cache,
    qall, pall, xall, kg, scores,
    stage, pst, agbuf, keybuf, xa, xown, qbuf, wt, cbuf, rows, dst, kbf, posv, poss,
    csem, ksem, lsem, ss, rs, kss, krs, zss, zrs,
):
    at = Place()
    loads = []
    for i in range(8):
        cols = pl.ds(1024 * i, 1024)
        loads.append(pltpu.make_async_copy(cache.at[:, cols], cbuf.at[:, cols], csem.at[i]))
        loads[-1].start()
    own_q = pltpu.make_async_copy(aq, qall.at[at.c], lsem.at[1])
    own_q.start()
    load_keys = pltpu.make_async_copy(keys, keybuf, lsem.at[3])
    load_keys.start()

    stage[...] = jnp.zeros_like(stage)
    for j in range(IHEADS):
        stage[pl.ds(j, 2, stride=128), :] = iq[:, 128 * j : 128 * j + 128].astype(F32)
    for k in range(CHUNKS):
        stage[pl.ds(64 + k, 2, stride=128), :] = tok[:, 128 * k : 128 * k + 128].astype(F32)
    lane = lax.broadcasted_iota(jnp.int32, (2, 128), 1)
    table = jnp.zeros((2, 128), F32)
    for k in range(8):
        mine = (lane == ids[:, k : k + 1]) | (lane == ids[:, k : k + 1] + 16)
        table = table + jnp.where(mine, eg[:, k : k + 1], 0.0)
    high = table.astype(BF16).astype(F32)
    stage[pl.ds(120, 2, stride=128), :] = jnp.where(lane < 16, high, table - high)
    stage[pl.ds(121, 2, stride=128), 0:IHEADS] = iw[...].astype(F32)
    agbuf[at.c] = stage[...].reshape(2, 128, 128).astype(BF16)
    first_lane = lax.broadcasted_iota(jnp.int32, (1, 128), 1)
    for o in range(16):
        for h in (0, 1):
            for k in (0, 1):
                pst[o, 2 * h + k : 2 * h + k + 1, :] = tp[h, o : o + 1, 128 * k : 128 * k + 128] * PITCH
        pst[o, 4:5, :] = jnp.where(first_lane == 0, oc[0:1, o : o + 1], oc[1:2, o : o + 1])
        pst[o, 5:8, :] = jnp.zeros((3, 128), jnp.int32)
    at.greet()
    few = Post(kss, krs)
    quick = plane_gather(few, at, lambda i, h, q: agbuf.at[i, h] if q is None else agbuf.at[i, h, pl.ds(64 * q, 64)])
    next(quick)
    places = [few.send(pst.at[at.peer(k)[1]], posv.at[at.c], at.peer(k)) for k in range(1, 16)]
    own_pos = pltpu.make_async_copy(pst.at[at.c], posv.at[at.c], lsem.at[2])
    own_pos.start()
    own_q.wait()
    many = Post(ss, rs)
    big = plane_gather(
        many, at, lambda i, h, q: qall.at[i, h] if q is None else qall.at[i, h, pl.ds(HALF * q, HALF)]
    )
    next(big)

    eye = (
        lax.broadcasted_iota(jnp.int32, (256, 256), 0) == lax.broadcasted_iota(jnp.int32, (256, 256), 1)
    ).astype(BF16)

    def turn_rows(i):
        loads[i].wait()

        def turn(b, _):
            off = pl.multiple_of(i * 1024 + b * 256, 256)
            t = lax.dot_general(
                eye, cbuf[:, pl.ds(off, 256)], (((1,), (1,)), ((), ())), preferred_element_type=F32
            )
            for c in range(5):
                w = min(128, WIDTH - 128 * c)
                rows[pl.ds(off * PITCH + c, 256, stride=PITCH), 0:w] = t[:, c * 128 : c * 128 + w]
            return 0

        lax.fori_loop(0, 4, turn, 0)

    turn_rows(0)
    next(quick)
    turn_rows(1)
    next(quick)
    turn_rows(2)
    next(quick)
    next(quick)
    next(quick)
    turn_rows(3)
    next(quick)
    next(big)
    turn_rows(4)
    for _ in quick:
        pass

    def widen(i, _):
        xa[pl.ds(pl.multiple_of(i * 256, 256), 256), :] = agbuf[i].reshape(256, 128).astype(F32)
        return 0

    lax.fori_loop(0, 16, widen, 0)

    def lay(k, _):
        xown[:, pl.ds(pl.multiple_of(k * 128, 128), 128)] = xa[pl.ds(64 + k, 32, stride=128), :].astype(BF16)
        return 0

    lax.fori_loop(0, CHUNKS + 1, lay, 0)
    zpost = Post(zss, zrs)
    up, down, over = (at.grp(1), at.c), (at.grp(-1), at.c), (at.grp(0, True), at.c)
    own_x = pltpu.make_async_copy(xown, xall.at[at.g], lsem.at[4])
    own_x.start()
    z_up = zpost.send(xown, xall.at[at.g], up)
    z_down = zpost.send(xown, xall.at[at.g], down)
    z_over = [zpost.send(xown, xall.at[at.g], over)]
    for cp in places:
        cp.wait_recv()
    own_pos.wait()
    to_smem = pltpu.make_async_copy(posv, poss, lsem.at[0])
    to_smem.start()
    keep_pos = pltpu.make_async_copy(posv, pall, lsem.at[2])
    keep_pos.start()

    def lay_q(j, _):
        qbuf[pl.ds(pl.multiple_of(j * 32, 32), 32), :] = xa[pl.ds(j, 32, stride=128), :].astype(BF16)
        return 0

    lax.fori_loop(0, IHEADS, lay_q, 0)
    wt[...] = jnp.concatenate([xa[pl.ds(121, 32, stride=128), :], jnp.zeros((96, 128), F32)], axis=0).T
    w = jnp.concatenate([wt[pl.ds(u, 16, stride=4), 0:32] for u in range(4)], axis=1)
    turn_rows(5)
    turn_rows(6)
    turn_rows(7)
    next(big)
    load_keys.wait()

    def index_block(b, _):
        k = keybuf[pl.ds(pl.multiple_of(b * KEYB, KEYB), KEYB), :]
        a = None
        for i in range(8):
            p = lax.dot_general(
                k, qbuf[i * 256 : i * 256 + 256, :], (((1,), (1,)), ((), ())), preferred_element_type=F32
            )
            for u in (0, 1):
                t = jnp.maximum(p[:, u * 128 : u * 128 + 128], 0.0) * w[2 * i + u : 2 * i + u + 1, :]
                a = t if a is None else a + t
        a = a + pltpu.roll(a, 64, 1)
        a = (a + pltpu.roll(a, 32, 1)).T
        n = KEYB // 128
        scale = kscale[pl.ds(pl.multiple_of(b * n, n), n), :]
        for j in range(n):
            cols = pl.ds(pl.multiple_of(b * KEYB + j * 128, 128), 128)
            scores[:, cols] = a[0:32, j * 128 : j * 128 + 128] * scale[j : j + 1, :]
        return 0

    def index(b):
        lax.fori_loop(b, b + 1, index_block, 0)

    index(0)
    next(big)
    index(1)
    next(big)
    z_up.wait_recv()
    low = xall.at[at.grp(-1)]
    z_low = zpost.send(low.at[pl.ds(0, 16)], low.at[pl.ds(0, 16)], up)
    z_over.append(zpost.send(low, low, over))
    z_down.wait_recv()
    high_x = xall.at[at.grp(1)]
    z_high = zpost.send(high_x.at[pl.ds(16, 16)], high_x.at[pl.ds(16, 16)], down)
    z_over.append(zpost.send(high_x, high_x, over))
    index(2)
    next(big)
    index(3)
    next(big)
    to_smem.wait()

    def select(t, _):
        c, line = t // 2, lax.rem(t, 2) * 2

        def pick(j, _):
            for u in range(64):
                p = poss[c, line + j // 2, lax.rem(j, 2) * 64 + u]
                dst[pl.ds((j * 64 + u) * PITCH, 8), :] = rows[pl.ds(p, 8), :]
            return 0

        lax.fori_loop(0, CAP // 64, pick, 0)
        for i in range(5):
            n = min(128, WIDTH - 128 * i)
            kbf[t, :, i * 128 : i * 128 + n] = dst[pl.ds(i, CAP, stride=PITCH), 0:n].astype(BF16)
        return 0

    keeps = []

    def select_rows(i):
        lax.fori_loop(8 * i, 8 * i + 8, select, 0)
        part = pl.ds(8 * i, 8)
        keeps.append(pltpu.make_async_copy(kbf.at[part], kg.at[part], ksem.at[i]))
        keeps[-1].start()

    select_rows(0)
    z_low.wait_recv()
    z_high.wait_recv()
    far = xall.at[at.grp(2)]
    z_over.append(zpost.send(far, far, over))
    select_rows(1)
    select_rows(2)
    select_rows(3)
    for _ in big:
        pass
    for cp in z_over:
        cp.wait_recv()
    for cp in keeps + [own_x, keep_pos]:
        cp.wait()
    for post in (few, many, zpost):
        post.finish()


def gather_all(*args):
    dma = pltpu.SemaphoreType.DMA
    return pl.pallas_call(
        gather_kernel,
        out_shape=(
            jax.ShapeDtypeStruct((16, 2, WIDTH, HEADS), BF16),
            jax.ShapeDtypeStruct((16, 8, 128), jnp.int32),
            jax.ShapeDtypeStruct((8, 32, TOKW), BF16),
            jax.ShapeDtypeStruct((32, CAP, WIDTH), BF16),
            jax.ShapeDtypeStruct((32, CACHE), F32),
        ),
        in_specs=[pl.BlockSpec(memory_space=VMEM)] * 8 + [pl.BlockSpec(memory_space=ANY)] * 3,
        out_specs=(pl.BlockSpec(memory_space=ANY),) * 4 + (pl.BlockSpec(memory_space=VMEM),),
        scratch_shapes=[
            VMEM((256, 128), F32),
            VMEM((16, 8, 128), jnp.int32),
            VMEM((16, 2, 128, 128), BF16),
            VMEM((CACHE, IDIM), BF16),
            VMEM((32 * 128, 128), F32),
            VMEM((32, TOKW), BF16),
            VMEM((IHEADS * 32, 128), BF16),
            VMEM((128, 128), F32),
            VMEM((WIDTH, CACHE), BF16),
            VMEM((CACHE * PITCH + 8, 128), F32),
            VMEM((CAP * PITCH + 8, 128), F32),
            VMEM((32, CAP, WIDTH), BF16),
            VMEM((16, 8, 128), jnp.int32),
            SMEM((16, 8, 128), jnp.int32),
            dma((8,)),
            dma((4,)),
            dma((5,)),
            dma((40,)),
            dma((40,)),
            dma((55,)),
            dma((55,)),
            dma((8,)),
            dma((8,)),
        ],
        compiler_params=pltpu.CompilerParams(collective_id=0, has_side_effects=True, vmem_limit_bytes=58 * 2**20),
    )(*args)


def merge(parts, lo, n):
    top = parts[0][1]
    for _, l in parts[1:]:
        top = jnp.maximum(top, l)
    es = [jnp.exp(l - top) for _, l in parts]
    tot = es[0]
    for e in es[1:]:
        tot = tot + e
    inv = 1.0 / tot
    diag = lax.broadcasted_iota(jnp.int32, (n, HEADS), 0) + lo == lax.broadcasted_iota(jnp.int32, (n, HEADS), 1)
    out = None
    for (o, _), e in zip(parts, es):
        w = jnp.broadcast_to((e * inv)[0:1], (n, HEADS))
        col = jnp.sum(jnp.where(diag, w, 0.0), axis=1, keepdims=True)
        term = o.astype(F32) * col
        out = term if out is None else out + term
    return out.astype(BF16), top + jnp.log(tot)


def attend_rows(at, counts, kbuf, qbuf, o, l, h, d):
    ids = [at.ctx(1 - h, d, e) for e in range(4)]
    ss = [jnp.dot(kbuf[2 * i + h], qbuf[i, h], preferred_element_type=F32) * SCALE for i in ids]
    ps = []
    for i, s in zip(ids, ss):
        live = lax.broadcasted_iota(jnp.int32, (CAP, HEADS), 0) < counts[i, 4, h]
        s = jnp.where(live, s, -1e30)
        m = jnp.max(s, axis=0, keepdims=True)
        e = jnp.where(live, jnp.exp(s - m), 0.0)
        n = jnp.sum(e, axis=0, keepdims=True)
        l[i, h] = jnp.broadcast_to(m + jnp.log(n), (8, HEADS))
        ps.append((e * (1.0 / n)).astype(BF16))
    for i, p in zip(ids, ps):
        v = kbuf[2 * i + h, :, 0:LATENT]
        o[i, h] = lax.dot_general(p, v, (((0,), (0,)), ((), ())), preferred_element_type=F32).astype(BF16)


def plane_scatter(post, at, work, o, l, bufs, result):
    r1, l1, m1, ml1, r2, l2, p1, pl1, r3, l3, m2, ml2, r4, l4 = bufs

    def both(src, lsrc, dst, ldst, dev):
        return post.send(src, dst, dev), post.send(lsrc, ldst, dev)

    def arrive(pair):
        for cp in pair:
            cp.wait_recv()

    s1, s2 = {}, {}
    for h in (0, 1):
        a = 1 - h
        work(h, 2)
        for e in range(4):
            i = at.ctx(a, 2, e)
            s1[h, e] = both(o.at[i, h], l.at[i, h], r1.at[h, e], l1.at[h, e], at.near(a, 1 if e < 2 else -1))
    yield
    for h in (0, 1):
        a = 1 - h
        work(h, 1)
        work(h, -1)
        for e in range(4):
            d = 0 if e >= 2 else 1
            i = at.ctx(a, 1 - 2 * d, e)
            s2[h, d, e] = both(o.at[i, h], l.at[i, h], r2.at[h, d, e], l2.at[h, d, e], at.near(a, 1 - 2 * d))
    yield
    for e in (0, 2, 1, 3):
        for h in (0, 1):
            a = 1 - h
            d = 0 if e < 2 else 1
            i = at.ctx(a, 1 - 2 * d, e)
            arrive(s1[h, e])
            m1[h, e], ml1[h, e] = merge([(o[i, h], l[i, h]), (r1[h, e], l1[h, e])], 0, HEADS)
            s2[h, d, e] = both(m1.at[h, e], ml1.at[h, e], r2.at[h, d, e], l2.at[h, d, e], at.near(a, 1 - 2 * d))
        if e == 2:
            yield
    work(0, 0)
    work(1, 0)
    yield
    s3, s4 = {}, {}
    for e in (2, 1, 3, 0):
        for h in (0, 1):
            a = 1 - h
            i = at.ctx(a, 0, e)
            arrive(s2[h, 0, e])
            arrive(s2[h, 1, e])
            p1[h, e], pl1[h, e] = merge(
                [(o[i, h], l[i, h]), (r2[h, 0, e], l2[h, 0, e]), (r2[h, 1, e], l2[h, 1, e])], 0, HEADS
            )
            if e == 2:
                for d in (0, 1):
                    s3[h, d] = both(
                        p1.at[h, 2, pl.ds(64 * d, 64)], pl1.at[h, 2], r3.at[h, d], l3.at[h, d], at.near(h, 1 - 2 * d)
                    )
        yield
    for h in (0, 1):
        for d in (0, 1):
            e = 1 if d == 0 else 3
            arrive(s3[h, d])
            mine = slice(64 * d, 64 * d + 64)
            rest = slice(64 - 64 * d, 128 - 64 * d)
            m2[h, d, rest] = p1[h, e, rest]
            m2[h, d, mine], lm = merge([(p1[h, e, mine], pl1[h, e]), (r3[h, d], l3[h, d])], 64 * d, 64)
            lane = lax.broadcasted_iota(jnp.int32, (8, HEADS), 1)
            ml2[h, d] = jnp.where((lane < 64) if d == 0 else (lane >= 64), lm, pl1[h, e])
            s4[h, d] = both(m2.at[h, d], ml2.at[h, d], r4.at[h, d], l4.at[h, d], at.near(h, 1 - 2 * d))
    yield
    for h in (0, 1):
        arrive(s4[h, 0])
        arrive(s4[h, 1])
        result[h], _ = merge([(p1[h, 0], pl1[h, 0]), (r4[h, 0], l4[h, 0]), (r4[h, 1], l4[h, 1])], 0, HEADS)


def reduce_kernel(
    counts, kg, qall, xall, gate, up, dn,
    attn, moe,
    kbuf, qbuf, o, l, tot,
    xbuf, wgu, dnbuf, acc, hid, mp, rc, rz1, rz2, yf, yb, ry,
    r1, l1, m1, ml1, r2, l2, p1, pl1, r3, l3, m2, ml2, r4, l4,
    rsem, lsem, ss, rs, zss, zrs,
):
    at = Place()
    near = {}
    for dx, dy in [(2, 2), (0, 2), (1, 2), (3, 2), (2, 0), (2, 1), (2, 3)] + [
        (dx, dy) for dx in (0, 1, 3) for dy in (0, 1, 3)
    ]:
        i = at.ctx(0, dx, dy)
        n = len(near)
        pair = pl.ds(2 * i, 2)
        near[dx, dy] = [
            pltpu.make_async_copy(kg.at[pair], kbuf.at[pair], rsem.at[2 * n]),
            pltpu.make_async_copy(qall.at[i], qbuf.at[i], rsem.at[2 * n + 1]),
        ]
        for cp in near[dx, dy]:
            cp.start()

    def work(h, d):
        for e in range(4):
            for cp in near.pop((e, d % 4) if h == 0 else (d % 4, e), ()):
                cp.wait()
        attend_rows(at, counts, kbuf, qbuf, o, l, h, d)

    loads = [pltpu.make_async_copy(xall, xbuf, lsem.at[0])]
    for e in (0, 1):
        loads.append(pltpu.make_async_copy(gate.at[e], wgu.at[e, :, pl.ds(0, 128)], lsem.at[1 + e]))
        loads.append(pltpu.make_async_copy(up.at[e], wgu.at[e, :, pl.ds(128, 128)], lsem.at[3 + e]))
    load_dn = pltpu.make_async_copy(dn, dnbuf, lsem.at[5])
    for cp in loads + [load_dn]:
        cp.start()
    at.greet()
    post = Post(ss, rs)
    flow = plane_scatter(post, at, work, o, l, (r1, l1, m1, ml1, r2, l2, p1, pl1, r3, l3, m2, ml2, r4, l4), attn)
    next(flow)

    for cp in loads:
        cp.wait()
    acc[...] = jnp.zeros_like(acc)

    def expand(k, _):
        cols = pl.ds(pl.multiple_of(k * 1024, 1024), 1024)
        x = xbuf[:, :, cols].reshape(256, 1024)
        for e in (0, 1):
            acc[e] += jnp.dot(x, wgu[e, cols, :], preferred_element_type=F32)
        return 0

    lax.fori_loop(0, MODEL // 1024, expand, 0)
    next(flow)
    gates = xbuf[:, :, MODEL:TOKW].reshape(256, 128).astype(F32)
    lane = lax.broadcasted_iota(jnp.int32, (256, 128), 1)
    for e in (0, 1):
        own = at.g * 2 + e
        col = jnp.sum(jnp.where((lane == own) | (lane == own + 16), gates, 0.0), axis=1, keepdims=True)
        gp, upart = acc[e, :, 0:128], acc[e, :, 128:256]
        hid[:, e * 128 : e * 128 + 128] = (gp / (1.0 + jnp.exp(-gp)) * upart * col).astype(BF16)
    load_dn.wait()

    def contract(k, _):
        cols = pl.ds(pl.multiple_of(k * 1024, 1024), 1024)
        mp[:, :, cols] = jnp.dot(hid[...], dnbuf[:, cols], preferred_element_type=F32).astype(BF16).reshape(8, 32, 1024)
        return 0

    lax.fori_loop(0, MODEL // 1024, contract, 0)
    zpost = Post(zss, zrs)
    zup, zdown, over = (at.grp(1), at.c), (at.grp(-1), at.c), (at.grp(0, True), at.c)
    order = (2, 1, -1, 0)
    swaps = [zpost.send(mp.at[at.grp(d, True)], rc.at[i], over) for i, d in enumerate(order)]
    next(flow)
    next(flow)

    def add(i, d):
        swaps[i].wait_recv()
        b = at.grp(d)
        mp[b] = (mp[b].astype(F32) + rc[i].astype(F32)).astype(BF16)

    add(0, 2)
    far = mp.at[at.grp(2)]
    za = zpost.send(far.at[pl.ds(0, 16)], rz1.at[0], zup)
    zb = zpost.send(far.at[pl.ds(16, 16)], rz1.at[1], zdown)
    next(flow)
    add(1, 1)
    add(2, -1)
    next(flow)
    za.wait_recv()
    b = at.grp(1)
    mp[b, 0:16] = (mp[b, 0:16].astype(F32) + rz1[0].astype(F32)).astype(BF16)
    zc = zpost.send(mp.at[b], rz2.at[0], zup)
    zb.wait_recv()
    b2 = at.grp(-1)
    mp[b2, 16:32] = (mp[b2, 16:32].astype(F32) + rz1[1].astype(F32)).astype(BF16)
    zd = zpost.send(mp.at[b2], rz2.at[1], zdown)
    swaps[3].wait_recv()
    next(flow)
    next(flow)
    zc.wait_recv()
    zd.wait_recv()

    def spread(k, _):
        cols = pl.ds(pl.multiple_of(k * 128, 128), 128)
        t = mp[at.g, :, cols].astype(F32) + rc[3, :, cols].astype(F32)
        t = t + rz2[0, :, cols].astype(F32) + rz2[1, :, cols].astype(F32)
        yf[pl.ds(k, 32, stride=CHUNKS), :] = t
        return 0

    lax.fori_loop(0, CHUNKS, spread, 0)

    def narrow(i, _):
        yb[i] = yf[pl.ds(pl.multiple_of(i * 112, 8), 112), :].astype(BF16)
        return 0

    lax.fori_loop(0, 16, narrow, 0)
    home = [zpost.send(yb.at[at.peer(k)[1]], ry.at[k - 1], at.peer(k)) for k in range(1, 16)]
    for _ in flow:
        pass
    total = yb[at.c].astype(F32)
    for k, cp in enumerate(home):
        cp.wait_recv()
        total = total + ry[k].astype(F32)
    tot[...] = total
    for k in range(CHUNKS):
        moe[:, 128 * k : 128 * k + 128] = tot[pl.ds(k, 2, stride=CHUNKS), :].astype(BF16)
    post.finish()
    zpost.finish()


def reduce_all(*args):
    dma = pltpu.SemaphoreType.DMA
    ob, lb = (HEADS, LATENT), (8, HEADS)

    def pair(*lead, block=ob):
        return [VMEM(lead + block, BF16), VMEM(lead + lb, F32)]

    return pl.pallas_call(
        reduce_kernel,
        out_shape=(jax.ShapeDtypeStruct((2, HEADS, LATENT), BF16), jax.ShapeDtypeStruct((2, MODEL), BF16)),
        in_specs=[pl.BlockSpec(memory_space=SMEM)] + [pl.BlockSpec(memory_space=ANY)] * 6,
        out_specs=(pl.BlockSpec(memory_space=VMEM),) * 2,
        scratch_shapes=[
            VMEM((32, CAP, WIDTH), BF16),
            VMEM((16, 2, WIDTH, HEADS), BF16),
            VMEM((16, 2) + ob, BF16),
            VMEM((16, 2) + lb, F32),
            VMEM((112, 128), F32),
            VMEM((8, 32, TOKW), BF16),
            VMEM((2, MODEL, 256), BF16),
            VMEM((256, MODEL), BF16),
            VMEM((2, 256, 256), F32),
            VMEM((256, 256), BF16),
            VMEM((8, 32, MODEL), BF16),
            VMEM((4, 32, MODEL), BF16),
            VMEM((2, 16, MODEL), BF16),
            VMEM((2, 32, MODEL), BF16),
            VMEM((32 * CHUNKS, 128), F32),
            VMEM((16, 112, 128), BF16),
            VMEM((15, 112, 128), BF16),
            *pair(2, 4),
            *pair(2, 4),
            *pair(2, 2, 4),
            *pair(2, 4),
            *pair(2, 2, block=(64, LATENT)),
            *pair(2, 2),
            *pair(2, 2),
            dma((32,)),
            dma((6,)),
            dma((64,)),
            dma((64,)),
            dma((23,)),
            dma((23,)),
        ],
        compiler_params=pltpu.CompilerParams(collective_id=1, has_side_effects=True, vmem_limit_bytes=58 * 2**20),
    )(*args)


def local(
    index_query, index_weights, index_keys, key_scales, attn_query, compact_cache, top_pos, owner_counts,
    moe_input, expert_ids, expert_gates, gate_proj, up_proj, down_proj,
):
    qall, pall, xall, kg, index_scores = gather_all(
        index_query, index_weights, moe_input, expert_ids, expert_gates, top_pos, owner_counts,
        key_scales.reshape(CACHE // 128, 128), jnp.swapaxes(attn_query, 1, 2), index_keys, compact_cache.T,
    )
    attn_out, moe_out = reduce_all(
        pall, kg, qall, xall, gate_proj, up_proj, down_proj.reshape(256, MODEL)
    )
    return index_scores, attn_out, moe_out


def solution(mesh):
    one = P(("grp", "ctx"))
    in_specs = (one,) * 11 + (P("grp", None, "ctx"), P("grp", None, "ctx"), P("grp", "ctx", None))
    return jax.shard_map(
        local, mesh=mesh, in_specs=in_specs, out_specs=(P("grp", "ctx"), one, one), check_vma=False
    )
```

```python
import jax
import jax.numpy as jnp
from jax import lax
from jax.experimental import pallas as pl
from jax.experimental.pallas import tpu as pltpu
from jax.sharding import PartitionSpec as P

MESH = pl.DeviceIdType.MESH
BF16, F32 = jnp.bfloat16, jnp.float32
HEADS, LATENT, WIDTH = 128, 512, 576
IHEADS, IDIM = 64, 128
CACHE, CAP = 8192, 256
MODEL = 7168
CHUNKS = MODEL // 128
TOKW = MODEL + 128
HALF = 288
KEYB = 2048
PITCH = 5
SCALE = 192.0**-0.5
ANY, VMEM, SMEM = pl.ANY, pltpu.VMEM, pltpu.SMEM


class Place:
    def __init__(self):
        self.g, self.c = lax.axis_index("grp"), lax.axis_index("ctx")
        self.z, self.core = self.g // 2, lax.rem(self.g, 2)
        self.x, self.y = self.c // 4, lax.rem(self.c, 4)

    def ctx(self, axis, d, e=0):
        dx, dy = (d, e) if axis == 0 else (e, d)
        return lax.rem(self.x + dx + 4, 4) * 4 + lax.rem(self.y + dy + 4, 4)

    def near(self, axis, d):
        return (self.g, self.ctx(axis, d))

    def peer(self, k):
        return (self.g, lax.rem(self.c + k, 16))

    def grp(self, d, other=False):
        core = 1 - self.core if other else self.core
        return lax.rem(self.z + d + 4, 4) * 2 + core

    def greet(self):
        bar = pltpu.get_barrier_semaphore()
        friends = [self.peer(k) for k in range(1, 16)]
        friends += [(self.grp(1), self.c), (self.grp(-1), self.c), (self.grp(0, True), self.c)]
        for f in friends:
            pl.semaphore_signal(bar, inc=1, device_id=f, device_id_type=MESH)
        pl.semaphore_wait(bar, len(friends))


class Post:
    def __init__(self, send_sems, recv_sems):
        self.ss, self.rs, self.out = send_sems, recv_sems, []

    def send(self, src, dst, dev):
        i = len(self.out)
        cp = pltpu.make_async_remote_copy(
            src_ref=src, dst_ref=dst, send_sem=self.ss.at[i], recv_sem=self.rs.at[i], device_id=dev, device_id_type=MESH
        )
        cp.start()
        self.out.append(cp)
        return cp

    def finish(self):
        for cp in self.out:
            cp.wait_send()


def plane_gather(post, at, part):
    def both(ref, axis):
        return post.send(ref, ref, at.near(axis, 1)), post.send(ref, ref, at.near(axis, -1))

    def split(src, h, axis, plus, minus):
        plus.wait_recv()
        lo = part(src(-1), h, 0)
        a = post.send(lo, lo, at.near(axis, 1))
        minus.wait_recv()
        hi = part(src(1), h, 1)
        return a, post.send(hi, hi, at.near(axis, -1))

    first = [both(part(at.c, h, None), h) for h in (0, 1)]
    across = {(h, 0): both(part(at.c, h, None), 1 - h) for h in (0, 1)}
    yield
    second = []
    for h in (0, 1):
        second.append(split(lambda d: at.ctx(h, d), h, h, *first[h]))
        for d in (-1, 1):
            across[h, d] = both(part(at.ctx(h, d), h, None), 1 - h)
    yield
    for h in (0, 1):
        for cp in second[h]:
            cp.wait_recv()
        across[h, 2] = both(part(at.ctx(h, 2), h, None), 1 - h)
    last = []
    for d in (0, -1, 1, 2):
        yield
        for h in (0, 1):
            last += split(lambda e: at.ctx(h, d, e), h, 1 - h, *across[h, d])
    yield
    for cp in last:
        cp.wait_recv()


def gather_kernel(
    iq, iw, tok, ids, eg, tp, oc, kscale, aq, keys, cache,
    qall, pall, xall, kg, scores,
    stage, pst, agbuf, keybuf, xa, xown, qbuf, wt, wq, cbuf, rows, dst, kbf, posv, poss,
    csem, ksem, lsem, ss, rs, kss, krs, zss, zrs,
):
    at = Place()
    loads = []
    for i in range(8):
        cols = pl.ds(1024 * i, 1024)
        loads.append(pltpu.make_async_copy(cache.at[:, cols], cbuf.at[:, cols], csem.at[i]))
        loads[-1].start()
    own_q = pltpu.make_async_copy(aq, qall.at[at.c], lsem.at[1])
    own_q.start()
    load_keys = pltpu.make_async_copy(keys, keybuf, lsem.at[3])
    load_keys.start()

    stage[...] = jnp.zeros_like(stage)
    for j in range(IHEADS):
        stage[pl.ds(j, 2, stride=128), :] = iq[:, 128 * j : 128 * j + 128].astype(F32)
    for k in range(CHUNKS):
        stage[pl.ds(64 + k, 2, stride=128), :] = tok[:, 128 * k : 128 * k + 128].astype(F32)
    lane = lax.broadcasted_iota(jnp.int32, (2, 128), 1)
    table = jnp.zeros((2, 128), F32)
    for k in range(8):
        mine = (lane == ids[:, k : k + 1]) | (lane == ids[:, k : k + 1] + 16)
        table = table + jnp.where(mine, eg[:, k : k + 1], 0.0)
    high = table.astype(BF16).astype(F32)
    stage[pl.ds(120, 2, stride=128), :] = jnp.where(lane < 16, high, table - high)
    stage[pl.ds(121, 2, stride=128), 0:IHEADS] = iw[...].astype(F32)
    agbuf[at.c] = stage[...].reshape(2, 128, 128).astype(BF16)
    first_lane = lax.broadcasted_iota(jnp.int32, (1, 128), 1)
    for o in range(16):
        for h in (0, 1):
            for k in (0, 1):
                pst[o, 2 * h + k : 2 * h + k + 1, :] = tp[h, o : o + 1, 128 * k : 128 * k + 128] * PITCH
        pst[o, 4:5, :] = jnp.where(first_lane == 0, oc[0:1, o : o + 1], oc[1:2, o : o + 1])
        pst[o, 5:8, :] = jnp.zeros((3, 128), jnp.int32)
    at.greet()
    few = Post(kss, krs)
    quick = plane_gather(few, at, lambda i, h, q: agbuf.at[i, h] if q is None else agbuf.at[i, h, pl.ds(64 * q, 64)])
    next(quick)
    places = [few.send(pst.at[at.peer(k)[1]], posv.at[at.c], at.peer(k)) for k in range(1, 16)]
    own_pos = pltpu.make_async_copy(pst.at[at.c], posv.at[at.c], lsem.at[2])
    own_pos.start()
    own_q.wait()
    many = Post(ss, rs)
    big = plane_gather(
        many, at, lambda i, h, q: qall.at[i, h] if q is None else qall.at[i, h, pl.ds(HALF * q, HALF)]
    )
    next(big)

    eye = (
        lax.broadcasted_iota(jnp.int32, (256, 256), 0) == lax.broadcasted_iota(jnp.int32, (256, 256), 1)
    ).astype(BF16)

    def turn_rows(i):
        loads[i].wait()

        for b in range(4):
            off = i * 1024 + b * 256
            x = cbuf[:, off : off + 256]
            if b < 3:
                t = x.T.astype(F32)
            else:
                t = lax.dot_general(eye, x, (((1,), (1,)), ((), ())), preferred_element_type=F32)
            for c in range(5):
                w = min(128, WIDTH - 128 * c)
                rows[pl.ds(off * PITCH + c, 256, stride=PITCH), 0:w] = t[:, c * 128 : c * 128 + w]

    def select(t, _):
        c, line = t // 2, lax.rem(t, 2) * 2
        for u in range(CAP):
            p = poss[c, line + u // 128, u % 128]
            dst[pl.ds(u * PITCH, 8), :] = rows[pl.ds(p, 8), :]
        for i in range(5):
            n = min(128, WIDTH - 128 * i)
            kbf[t, :, i * 128 : i * 128 + n] = dst[pl.ds(i, CAP, stride=PITCH), 0:n].astype(BF16)
        return 0

    keeps = []

    def select_rows(i):
        lax.fori_loop(8 * i, 8 * i + 8, select, 0)
        part = pl.ds(8 * i, 8)
        keeps.append(pltpu.make_async_copy(kbf.at[part], kg.at[part], ksem.at[i]))
        keeps[-1].start()

    for i in range(4):
        turn_rows(i)
    next(quick)
    for i in range(4, 8):
        turn_rows(i)
    for cp in places:
        cp.wait_recv()
    own_pos.wait()
    to_smem = pltpu.make_async_copy(posv, poss, lsem.at[0])
    to_smem.start()
    keep_pos = pltpu.make_async_copy(posv, pall, lsem.at[2])
    keep_pos.start()
    next(quick)
    next(big)
    to_smem.wait()
    next(quick)
    select_rows(0)
    next(quick)
    next(quick)
    next(quick)
    select_rows(1)
    for _ in quick:
        pass
    next(big)

    def widen(i, _):
        xa[pl.ds(pl.multiple_of(i * 256, 256), 256), :] = agbuf[i].reshape(256, 128).astype(F32)
        return 0

    lax.fori_loop(0, 16, widen, 0)

    def lay(k, _):
        for u in range(3):
            cols = pl.ds(pl.multiple_of(k * 384 + u * 128, 128), 128)
            xown[:, cols] = xa[pl.ds(64 + 3 * k + u, 32, stride=128), :].astype(BF16)
        return 0

    lax.fori_loop(0, (CHUNKS + 1) // 3, lay, 0)
    zpost = Post(zss, zrs)
    up, down, over = (at.grp(1), at.c), (at.grp(-1), at.c), (at.grp(0, True), at.c)
    own_x = pltpu.make_async_copy(xown, xall.at[at.g], lsem.at[4])
    own_x.start()
    z_up = zpost.send(xown, xall.at[at.g], up)
    z_down = zpost.send(xown, xall.at[at.g], down)
    z_over = [zpost.send(xown, xall.at[at.g], over)]
    def lay_q(j, _):
        for u in range(4):
            qbuf[pl.ds(pl.multiple_of(j * 128 + u * 32, 32), 32), :] = xa[pl.ds(4 * j + u, 32, stride=128), :].astype(BF16)
        return 0

    lax.fori_loop(0, IHEADS // 4, lay_q, 0)
    wt[...] = jnp.concatenate([xa[pl.ds(121, 32, stride=128), :], jnp.zeros((96, 128), F32)], axis=0).T
    wq[...] = jnp.concatenate([wt[pl.ds(u, 16, stride=4), 0:32] for u in range(4)], axis=1)
    select_rows(2)
    next(big)
    load_keys.wait()

    def index_block(b, _):
        k = keybuf[pl.ds(pl.multiple_of(b * KEYB, KEYB), KEYB), :]
        a = None
        for i in range(8):
            p = lax.dot_general(
                k, qbuf[i * 256 : i * 256 + 256, :], (((1,), (1,)), ((), ())), preferred_element_type=F32
            )
            for u in (0, 1):
                t = jnp.maximum(p[:, u * 128 : u * 128 + 128], 0.0) * wq[2 * i + u : 2 * i + u + 1, :]
                a = t if a is None else a + t
        a = a + pltpu.roll(a, 64, 1)
        a = (a + pltpu.roll(a, 32, 1)).T
        n = KEYB // 128
        scale = kscale[pl.ds(pl.multiple_of(b * n, n), n), :]
        for j in range(n):
            cols = pl.ds(pl.multiple_of(b * KEYB + j * 128, 128), 128)
            scores[:, cols] = a[0:32, j * 128 : j * 128 + 128] * scale[j : j + 1, :]
        return 0

    def index(b):
        lax.fori_loop(b, b + 1, index_block, 0)

    index(0)
    next(big)
    index(1)
    z_up.wait_recv()
    low = xall.at[at.grp(-1)]
    z_low = zpost.send(low.at[pl.ds(0, 16)], low.at[pl.ds(0, 16)], up)
    z_over.append(zpost.send(low, low, over))
    z_down.wait_recv()
    high_x = xall.at[at.grp(1)]
    z_high = zpost.send(high_x.at[pl.ds(16, 16)], high_x.at[pl.ds(16, 16)], down)
    z_over.append(zpost.send(high_x, high_x, over))
    next(big)
    index(2)
    next(big)
    select_rows(3)
    z_low.wait_recv()
    z_high.wait_recv()
    far = xall.at[at.grp(2)]
    z_over.append(zpost.send(far, far, over))
    index(3)
    for _ in big:
        pass
    for cp in z_over:
        cp.wait_recv()
    for cp in keeps + [own_x, keep_pos]:
        cp.wait()
    for post in (few, many, zpost):
        post.finish()


def gather_all(*args):
    dma = pltpu.SemaphoreType.DMA
    return pl.pallas_call(
        gather_kernel,
        out_shape=(
            jax.ShapeDtypeStruct((16, 2, WIDTH, HEADS), BF16),
            jax.ShapeDtypeStruct((16, 8, 128), jnp.int32),
            jax.ShapeDtypeStruct((8, 32, TOKW), BF16),
            jax.ShapeDtypeStruct((32, CAP, WIDTH), BF16),
            jax.ShapeDtypeStruct((32, CACHE), F32),
        ),
        in_specs=[pl.BlockSpec(memory_space=VMEM)] * 8 + [pl.BlockSpec(memory_space=ANY)] * 3,
        out_specs=(pl.BlockSpec(memory_space=ANY),) * 4 + (pl.BlockSpec(memory_space=VMEM),),
        scratch_shapes=[
            VMEM((256, 128), F32),
            VMEM((16, 8, 128), jnp.int32),
            VMEM((16, 2, 128, 128), BF16),
            VMEM((CACHE, IDIM), BF16),
            VMEM((32 * 128, 128), F32),
            VMEM((32, TOKW), BF16),
            VMEM((IHEADS * 32, 128), BF16),
            VMEM((128, 128), F32),
            VMEM((16, 128), F32),
            VMEM((WIDTH, CACHE), BF16),
            VMEM((CACHE * PITCH + 8, 128), F32),
            VMEM((CAP * PITCH + 8, 128), F32),
            VMEM((32, CAP, WIDTH), BF16),
            VMEM((16, 8, 128), jnp.int32),
            SMEM((16, 8, 128), jnp.int32),
            dma((8,)),
            dma((4,)),
            dma((5,)),
            dma((40,)),
            dma((40,)),
            dma((55,)),
            dma((55,)),
            dma((8,)),
            dma((8,)),
        ],
        compiler_params=pltpu.CompilerParams(collective_id=0, has_side_effects=True, vmem_limit_bytes=58 * 2**20),
    )(*args)


def merge(parts, lo, n):
    top = parts[0][1]
    for _, l in parts[1:]:
        top = jnp.maximum(top, l)
    es = [jnp.exp(l - top) for _, l in parts]
    tot = es[0]
    for e in es[1:]:
        tot = tot + e
    inv = 1.0 / tot
    diag = lax.broadcasted_iota(jnp.int32, (n, HEADS), 0) + lo == lax.broadcasted_iota(jnp.int32, (n, HEADS), 1)
    out = None
    for (o, _), e in zip(parts, es):
        w = jnp.broadcast_to((e * inv)[0:1], (n, HEADS))
        col = jnp.sum(jnp.where(diag, w, 0.0), axis=1, keepdims=True)
        term = o.astype(F32) * col
        out = term if out is None else out + term
    return out.astype(BF16), top + jnp.log(tot)


def attend_rows(at, counts, kbuf, qbuf, o, l, h, d):
    ids = [at.ctx(1 - h, d, e) for e in range(4)]
    ss = [jnp.dot(kbuf[2 * i + h], qbuf[i, h], preferred_element_type=F32) * SCALE for i in ids]
    ps = []
    for i, s in zip(ids, ss):
        live = lax.broadcasted_iota(jnp.int32, (CAP, HEADS), 0) < counts[i, 4, h]
        s = jnp.where(live, s, -1e30)
        m = jnp.max(s, axis=0, keepdims=True)
        e = jnp.where(live, jnp.exp(s - m), 0.0)
        n = jnp.sum(e, axis=0, keepdims=True)
        l[i, h] = jnp.broadcast_to(m + jnp.log(n), (8, HEADS))
        ps.append((e * (1.0 / n)).astype(BF16))
    for i, p in zip(ids, ps):
        v = kbuf[2 * i + h, :, 0:LATENT]
        o[i, h] = lax.dot_general(p, v, (((0,), (0,)), ((), ())), preferred_element_type=F32).astype(BF16)


def plane_scatter(post, at, work, o, l, bufs, result):
    r1, l1, m1, ml1, r2, l2, p1, pl1, r3, l3, m2, ml2, r4, l4 = bufs

    def both(src, lsrc, dst, ldst, dev):
        return post.send(src, dst, dev), post.send(lsrc, ldst, dev)

    def arrive(pair):
        for cp in pair:
            cp.wait_recv()

    s1, s2 = {}, {}
    for h in (0, 1):
        a = 1 - h
        work(h, 2)
        for e in range(4):
            i = at.ctx(a, 2, e)
            s1[h, e] = both(o.at[i, h], l.at[i, h], r1.at[h, e], l1.at[h, e], at.near(a, 1 if e < 2 else -1))
    yield
    for h in (0, 1):
        a = 1 - h
        work(h, 1)
        work(h, -1)
        for e in range(4):
            d = 0 if e >= 2 else 1
            i = at.ctx(a, 1 - 2 * d, e)
            s2[h, d, e] = both(o.at[i, h], l.at[i, h], r2.at[h, d, e], l2.at[h, d, e], at.near(a, 1 - 2 * d))
    yield
    for e in (0, 2, 1, 3):
        for h in (0, 1):
            a = 1 - h
            d = 0 if e < 2 else 1
            i = at.ctx(a, 1 - 2 * d, e)
            arrive(s1[h, e])
            m1[h, e], ml1[h, e] = merge([(o[i, h], l[i, h]), (r1[h, e], l1[h, e])], 0, HEADS)
            s2[h, d, e] = both(m1.at[h, e], ml1.at[h, e], r2.at[h, d, e], l2.at[h, d, e], at.near(a, 1 - 2 * d))
        if e == 2:
            yield
    work(0, 0)
    work(1, 0)
    yield
    s3, s4 = {}, {}
    for e in (2, 1, 3, 0):
        for h in (0, 1):
            a = 1 - h
            i = at.ctx(a, 0, e)
            arrive(s2[h, 0, e])
            arrive(s2[h, 1, e])
            p1[h, e], pl1[h, e] = merge(
                [(o[i, h], l[i, h]), (r2[h, 0, e], l2[h, 0, e]), (r2[h, 1, e], l2[h, 1, e])], 0, HEADS
            )
            if e == 2:
                for d in (0, 1):
                    s3[h, d] = both(
                        p1.at[h, 2, pl.ds(64 * d, 64)], pl1.at[h, 2], r3.at[h, d], l3.at[h, d], at.near(h, 1 - 2 * d)
                    )
        yield
    for h in (0, 1):
        for d in (0, 1):
            e = 1 if d == 0 else 3
            arrive(s3[h, d])
            mine = slice(64 * d, 64 * d + 64)
            rest = slice(64 - 64 * d, 128 - 64 * d)
            m2[h, d, rest] = p1[h, e, rest]
            m2[h, d, mine], lm = merge([(p1[h, e, mine], pl1[h, e]), (r3[h, d], l3[h, d])], 64 * d, 64)
            lane = lax.broadcasted_iota(jnp.int32, (8, HEADS), 1)
            ml2[h, d] = jnp.where((lane < 64) if d == 0 else (lane >= 64), lm, pl1[h, e])
            s4[h, d] = both(m2.at[h, d], ml2.at[h, d], r4.at[h, d], l4.at[h, d], at.near(h, 1 - 2 * d))
    yield
    for h in (0, 1):
        arrive(s4[h, 0])
        arrive(s4[h, 1])
        result[h], _ = merge([(p1[h, 0], pl1[h, 0]), (r4[h, 0], l4[h, 0]), (r4[h, 1], l4[h, 1])], 0, HEADS)


def reduce_kernel(
    counts, kg, qall, xall, gate, up, dn,
    attn, moe,
    kbuf, qbuf, o, l, tot,
    xbuf, wgu, dnbuf, acc, hid, mp, rc, rz1, rz2, yf, yb, ry,
    r1, l1, m1, ml1, r2, l2, p1, pl1, r3, l3, m2, ml2, r4, l4,
    rsem, lsem, ss, rs, zss, zrs,
):
    at = Place()
    near = {}
    def fetch(dx, dy):
        i = at.ctx(0, dx, dy)
        n = len(near)
        pair = pl.ds(2 * i, 2)
        near[dx, dy] = [
            pltpu.make_async_copy(kg.at[pair], kbuf.at[pair], rsem.at[2 * n]),
            pltpu.make_async_copy(qall.at[i], qbuf.at[i], rsem.at[2 * n + 1]),
        ]
        for cp in near[dx, dy]:
            cp.start()

    for dx, dy in [(2, 2), (0, 2), (1, 2), (3, 2), (2, 0), (2, 1), (2, 3)]:
        fetch(dx, dy)

    def work(h, d):
        for e in range(4):
            for cp in near.pop((e, d % 4) if h == 0 else (d % 4, e), ()):
                cp.wait()
        attend_rows(at, counts, kbuf, qbuf, o, l, h, d)

    loads = [pltpu.make_async_copy(xall, xbuf, lsem.at[0])]
    for e in (0, 1):
        loads.append(pltpu.make_async_copy(gate.at[e], wgu.at[e, :, pl.ds(0, 128)], lsem.at[1 + e]))
        loads.append(pltpu.make_async_copy(up.at[e], wgu.at[e, :, pl.ds(128, 128)], lsem.at[3 + e]))
    load_dn = pltpu.make_async_copy(dn, dnbuf, lsem.at[5])
    for cp in loads + [load_dn]:
        cp.start()
    for dx, dy in [(dx, dy) for dx in (1, 3, 0) for dy in (1, 3, 0)]:
        fetch(dx, dy)
    at.greet()
    post = Post(ss, rs)
    flow = plane_scatter(post, at, work, o, l, (r1, l1, m1, ml1, r2, l2, p1, pl1, r3, l3, m2, ml2, r4, l4), attn)
    next(flow)

    for cp in loads:
        cp.wait()
    acc[...] = jnp.zeros_like(acc)

    def expand(k, _):
        cols = pl.ds(pl.multiple_of(k * 1024, 1024), 1024)
        x = xbuf[:, :, cols].reshape(256, 1024)
        for e in (0, 1):
            acc[e] += jnp.dot(x, wgu[e, cols, :], preferred_element_type=F32)
        return 0

    lax.fori_loop(0, MODEL // 1024, expand, 0)
    gates = xbuf[:, :, MODEL:TOKW].reshape(256, 128).astype(F32)
    lane = lax.broadcasted_iota(jnp.int32, (256, 128), 1)
    for e in (0, 1):
        own = at.g * 2 + e
        col = jnp.sum(jnp.where((lane == own) | (lane == own + 16), gates, 0.0), axis=1, keepdims=True)
        gp, upart = acc[e, :, 0:128], acc[e, :, 128:256]
        hid[:, e * 128 : e * 128 + 128] = (gp / (1.0 + jnp.exp(-gp)) * upart * col).astype(BF16)
    load_dn.wait()

    def contract(k, _):
        cols = pl.ds(pl.multiple_of(k * 1024, 1024), 1024)
        mp[:, :, cols] = jnp.dot(hid[...], dnbuf[:, cols], preferred_element_type=F32).astype(BF16).reshape(8, 32, 1024)
        return 0

    lax.fori_loop(0, MODEL // 1024, contract, 0)
    zpost = Post(zss, zrs)
    zup, zdown, over = (at.grp(1), at.c), (at.grp(-1), at.c), (at.grp(0, True), at.c)
    order = (2, 1, -1, 0)
    swaps = [zpost.send(mp.at[at.grp(d, True)], rc.at[i], over) for i, d in enumerate(order)]
    next(flow)

    def add(i, d):
        swaps[i].wait_recv()
        b = at.grp(d)
        mp[b] = (mp[b].astype(F32) + rc[i].astype(F32)).astype(BF16)
        return mp.at[b]

    low, top = pl.ds(0, 16), pl.ds(16, 16)
    far = add(0, 2)
    za = zpost.send(far.at[low], rz1.at[0], zup)
    zb = zpost.send(far.at[top], rz1.at[1], zdown)
    above = add(1, 1)
    zc = [zpost.send(above.at[top], rz2.at[0, top], zup)]
    below = add(2, -1)
    zd = [zpost.send(below.at[low], rz2.at[1, low], zdown)]
    next(flow)
    next(flow)
    za.wait_recv()
    above[0:16] = (above[0:16].astype(F32) + rz1[0].astype(F32)).astype(BF16)
    zc.append(zpost.send(above.at[low], rz2.at[0, low], zup))
    zb.wait_recv()
    below[16:32] = (below[16:32].astype(F32) + rz1[1].astype(F32)).astype(BF16)
    zd.append(zpost.send(below.at[top], rz2.at[1, top], zdown))
    swaps[3].wait_recv()
    for _ in range(5):
        next(flow)
    for cp in zc + zd:
        cp.wait_recv()

    def spread(k, _):
        cols = pl.ds(pl.multiple_of(k * 128, 128), 128)
        t = mp[at.g, :, cols].astype(F32) + rc[3, :, cols].astype(F32)
        t = t + rz2[0, :, cols].astype(F32) + rz2[1, :, cols].astype(F32)
        yf[pl.ds(k, 32, stride=CHUNKS), :] = t
        return 0

    lax.fori_loop(0, CHUNKS, spread, 0)

    def narrow(i, _):
        yb[i] = yf[pl.ds(pl.multiple_of(i * 112, 8), 112), :].astype(BF16)
        return 0

    lax.fori_loop(0, 16, narrow, 0)
    home = [zpost.send(yb.at[at.peer(k)[1]], ry.at[k - 1], at.peer(k)) for k in range(1, 16)]
    for _ in flow:
        pass
    total = yb[at.c].astype(F32)
    for k, cp in enumerate(home):
        cp.wait_recv()
        total = total + ry[k].astype(F32)
    tot[...] = total
    for k in range(CHUNKS):
        moe[:, 128 * k : 128 * k + 128] = tot[pl.ds(k, 2, stride=CHUNKS), :].astype(BF16)
    post.finish()
    zpost.finish()


def reduce_all(*args):
    dma = pltpu.SemaphoreType.DMA
    ob, lb = (HEADS, LATENT), (8, HEADS)

    def pair(*lead, block=ob):
        return [VMEM(lead + block, BF16), VMEM(lead + lb, F32)]

    return pl.pallas_call(
        reduce_kernel,
        out_shape=(jax.ShapeDtypeStruct((2, HEADS, LATENT), BF16), jax.ShapeDtypeStruct((2, MODEL), BF16)),
        in_specs=[pl.BlockSpec(memory_space=SMEM)] + [pl.BlockSpec(memory_space=ANY)] * 6,
        out_specs=(pl.BlockSpec(memory_space=VMEM),) * 2,
        scratch_shapes=[
            VMEM((32, CAP, WIDTH), BF16),
            VMEM((16, 2, WIDTH, HEADS), BF16),
            VMEM((16, 2) + ob, BF16),
            VMEM((16, 2) + lb, F32),
            VMEM((112, 128), F32),
            VMEM((8, 32, TOKW), BF16),
            VMEM((2, MODEL, 256), BF16),
            VMEM((256, MODEL), BF16),
            VMEM((2, 256, 256), F32),
            VMEM((256, 256), BF16),
            VMEM((8, 32, MODEL), BF16),
            VMEM((4, 32, MODEL), BF16),
            VMEM((2, 16, MODEL), BF16),
            VMEM((2, 32, MODEL), BF16),
            VMEM((32 * CHUNKS, 128), F32),
            VMEM((16, 112, 128), BF16),
            VMEM((15, 112, 128), BF16),
            *pair(2, 4),
            *pair(2, 4),
            *pair(2, 2, 4),
            *pair(2, 4),
            *pair(2, 2, block=(64, LATENT)),
            *pair(2, 2),
            *pair(2, 2),
            dma((32,)),
            dma((6,)),
            dma((64,)),
            dma((64,)),
            dma((25,)),
            dma((25,)),
        ],
        compiler_params=pltpu.CompilerParams(collective_id=1, has_side_effects=True, vmem_limit_bytes=58 * 2**20),
    )(*args)


def local(
    index_query, index_weights, index_keys, key_scales, attn_query, compact_cache, top_pos, owner_counts,
    moe_input, expert_ids, expert_gates, gate_proj, up_proj, down_proj,
):
    qall, pall, xall, kg, index_scores = gather_all(
        index_query, index_weights, moe_input, expert_ids, expert_gates, top_pos, owner_counts,
        key_scales.reshape(CACHE // 128, 128), jnp.swapaxes(attn_query, 1, 2), index_keys, compact_cache.T,
    )
    attn_out, moe_out = reduce_all(
        pall, kg, qall, xall, gate_proj, up_proj, down_proj.reshape(256, MODEL)
    )
    return index_scores, attn_out, moe_out


def solution(mesh):
    one = P(("grp", "ctx"))
    in_specs = (one,) * 11 + (P("grp", None, "ctx"), P("grp", None, "ctx"), P("grp", "ctx", None))
    return jax.shard_map(
        local, mesh=mesh, in_specs=in_specs, out_specs=(P("grp", "ctx"), one, one), check_vma=False
    )
```

```python
import jax
import jax.numpy as jnp
from jax import lax
from jax.experimental import pallas as pl
from jax.experimental.pallas import tpu as pltpu
from jax.sharding import PartitionSpec as P

MESH = pl.DeviceIdType.MESH
BF16, F32 = jnp.bfloat16, jnp.float32
HEADS, LATENT, WIDTH = 128, 512, 576
IHEADS, IDIM = 64, 128
CACHE, CAP = 8192, 256
MODEL = 7168
CHUNKS = MODEL // 128
TOKW = MODEL + 128
HALF = 288
KEYB = 2048
PITCH = 5
SCALE = 192.0**-0.5
ANY, VMEM, SMEM = pl.ANY, pltpu.VMEM, pltpu.SMEM


class Place:
    def __init__(self):
        self.g, self.c = lax.axis_index("grp"), lax.axis_index("ctx")
        self.z, self.core = self.g // 2, lax.rem(self.g, 2)
        self.x, self.y = self.c // 4, lax.rem(self.c, 4)

    def ctx(self, axis, d, e=0):
        dx, dy = (d, e) if axis == 0 else (e, d)
        return lax.rem(self.x + dx + 4, 4) * 4 + lax.rem(self.y + dy + 4, 4)

    def near(self, axis, d):
        return (self.g, self.ctx(axis, d))

    def peer(self, k):
        return (self.g, lax.rem(self.c + k, 16))

    def grp(self, d, other=False):
        core = 1 - self.core if other else self.core
        return lax.rem(self.z + d + 4, 4) * 2 + core

    def greet(self):
        bar = pltpu.get_barrier_semaphore()
        friends = [self.peer(k) for k in range(1, 16)]
        friends += [(self.grp(1), self.c), (self.grp(-1), self.c), (self.grp(0, True), self.c)]
        for f in friends:
            pl.semaphore_signal(bar, inc=1, device_id=f, device_id_type=MESH)
        pl.semaphore_wait(bar, len(friends))


class Post:
    def __init__(self, send_sems, recv_sems):
        self.ss, self.rs, self.out = send_sems, recv_sems, []

    def send(self, src, dst, dev):
        i = len(self.out)
        cp = pltpu.make_async_remote_copy(
            src_ref=src, dst_ref=dst, send_sem=self.ss.at[i], recv_sem=self.rs.at[i], device_id=dev, device_id_type=MESH
        )
        cp.start()
        self.out.append(cp)
        return cp

    def finish(self):
        for cp in self.out:
            cp.wait_send()


def plane_gather(post, at, own, part):
    def both(ref, axis, src=None):
        src = ref if src is None else src
        return post.send(src, ref, at.near(axis, 1)), post.send(src, ref, at.near(axis, -1))

    def split(src, h, axis, plus, minus):
        plus.wait_recv()
        lo = part(src(-1), h, 0)
        a = post.send(lo, lo, at.near(axis, 1))
        minus.wait_recv()
        hi = part(src(1), h, 1)
        return a, post.send(hi, hi, at.near(axis, -1))

    first = [both(part(at.c, h, None), h, own.at[h]) for h in (0, 1)]
    across = {(h, 0): both(part(at.c, h, None), 1 - h, own.at[h]) for h in (0, 1)}
    yield
    second = []
    for h in (0, 1):
        second.append(split(lambda d: at.ctx(h, d), h, h, *first[h]))
        for d in (-1, 1):
            across[h, d] = both(part(at.ctx(h, d), h, None), 1 - h)
    yield
    for h in (0, 1):
        for cp in second[h]:
            cp.wait_recv()
        across[h, 2] = both(part(at.ctx(h, 2), h, None), 1 - h)
    last = []
    for d in (0, -1, 1, 2):
        yield
        for h in (0, 1):
            last += split(lambda e: at.ctx(h, d, e), h, 1 - h, *across[h, d])
    yield
    for cp in last:
        cp.wait_recv()


def gather_kernel(
    iq, iw, tok, ids, eg, tp, oc, kscale, aq, keys, cache,
    qall, pall, xall, kg, scores,
    stage, pst, agbuf, keybuf, xa, xown, qbuf, wt, wq, cbuf, rows, dst, kbf, posv, poss,
    csem, ksem, lsem, ss, rs, kss, krs, zss, zrs,
):
    at = Place()
    loads = []
    for i in range(8):
        cols = pl.ds(1024 * i, 1024)
        loads.append(pltpu.make_async_copy(cache.at[:, cols], cbuf.at[:, cols], csem.at[i]))
        loads[-1].start()
    own_q = pltpu.make_async_copy(aq, qall.at[at.c], lsem.at[1])
    own_q.start()
    load_keys = pltpu.make_async_copy(keys, keybuf, lsem.at[3])
    load_keys.start()

    stage[...] = jnp.zeros_like(stage)
    for j in range(IHEADS):
        stage[pl.ds(j, 2, stride=128), :] = iq[:, 128 * j : 128 * j + 128].astype(F32)
    for k in range(CHUNKS):
        stage[pl.ds(64 + k, 2, stride=128), :] = tok[:, 128 * k : 128 * k + 128].astype(F32)
    lane = lax.broadcasted_iota(jnp.int32, (2, 128), 1)
    table = jnp.zeros((2, 128), F32)
    for k in range(8):
        mine = (lane == ids[:, k : k + 1]) | (lane == ids[:, k : k + 1] + 16)
        table = table + jnp.where(mine, eg[:, k : k + 1], 0.0)
    high = table.astype(BF16).astype(F32)
    stage[pl.ds(120, 2, stride=128), :] = jnp.where(lane < 16, high, table - high)
    stage[pl.ds(121, 2, stride=128), 0:IHEADS] = iw[...].astype(F32)
    agbuf[at.c] = stage[...].reshape(2, 128, 128).astype(BF16)
    first_lane = lax.broadcasted_iota(jnp.int32, (1, 128), 1)
    for o in range(16):
        for h in (0, 1):
            for k in (0, 1):
                pst[o, 2 * h + k : 2 * h + k + 1, :] = tp[h, o : o + 1, 128 * k : 128 * k + 128] * PITCH
        pst[o, 4:5, :] = jnp.where(first_lane == 0, oc[0:1, o : o + 1], oc[1:2, o : o + 1])
        pst[o, 5:8, :] = jnp.zeros((3, 128), jnp.int32)
    at.greet()
    few = Post(kss, krs)
    quick = plane_gather(
        few, at, agbuf.at[at.c], lambda i, h, q: agbuf.at[i, h] if q is None else agbuf.at[i, h, pl.ds(64 * q, 64)]
    )
    next(quick)
    places = [few.send(pst.at[at.peer(k)[1]], posv.at[at.c], at.peer(k)) for k in range(1, 16)]
    own_pos = pltpu.make_async_copy(pst.at[at.c], posv.at[at.c], lsem.at[2])
    own_pos.start()
    many = Post(ss, rs)
    big = plane_gather(
        many, at, aq, lambda i, h, q: qall.at[i, h] if q is None else qall.at[i, h, pl.ds(HALF * q, HALF)]
    )
    next(big)

    eye = (
        lax.broadcasted_iota(jnp.int32, (256, 256), 0) == lax.broadcasted_iota(jnp.int32, (256, 256), 1)
    ).astype(BF16)

    def turn_rows(i):
        loads[i].wait()

        for b in range(4):
            off = i * 1024 + b * 256
            x = cbuf[:, off : off + 256]
            if b < 3:
                t = x.T.astype(F32)
            else:
                t = lax.dot_general(eye, x, (((1,), (1,)), ((), ())), preferred_element_type=F32)
            for c in range(5):
                w = min(128, WIDTH - 128 * c)
                rows[pl.ds(off * PITCH + c, 256, stride=PITCH), 0:w] = t[:, c * 128 : c * 128 + w]

    def select(t, _):
        c, line = t // 2, lax.rem(t, 2) * 2
        for u in range(CAP):
            p = poss[c, line + u // 128, u % 128]
            dst[pl.ds(u * PITCH, 8), :] = rows[pl.ds(p, 8), :]
        for i in range(5):
            n = min(128, WIDTH - 128 * i)
            kbf[t, :, i * 128 : i * 128 + n] = dst[pl.ds(i, CAP, stride=PITCH), 0:n].astype(BF16)
        return 0

    keeps = []

    def select_rows(i):
        lax.fori_loop(8 * i, 8 * i + 8, select, 0)
        part = pl.ds(8 * i, 8)
        keeps.append(pltpu.make_async_copy(kbf.at[part], kg.at[part], ksem.at[i]))
        keeps[-1].start()

    for i in range(4):
        turn_rows(i)
    next(quick)
    for i in range(4, 8):
        turn_rows(i)
    for cp in places:
        cp.wait_recv()
    own_pos.wait()
    to_smem = pltpu.make_async_copy(posv, poss, lsem.at[0])
    to_smem.start()
    keep_pos = pltpu.make_async_copy(posv, pall, lsem.at[2])
    keep_pos.start()
    next(quick)
    next(big)
    to_smem.wait()
    next(quick)
    select_rows(0)
    next(quick)
    next(quick)
    next(quick)
    select_rows(1)
    for _ in quick:
        pass
    next(big)

    def widen(i, _):
        xa[pl.ds(pl.multiple_of(i * 256, 256), 256), :] = agbuf[i].reshape(256, 128).astype(F32)
        return 0

    lax.fori_loop(0, 16, widen, 0)

    def lay(k, _):
        for u in range(3):
            cols = pl.ds(pl.multiple_of(k * 384 + u * 128, 128), 128)
            xown[:, cols] = xa[pl.ds(64 + 3 * k + u, 32, stride=128), :].astype(BF16)
        return 0

    lax.fori_loop(0, (CHUNKS + 1) // 3, lay, 0)
    zpost = Post(zss, zrs)
    up, down, over = (at.grp(1), at.c), (at.grp(-1), at.c), (at.grp(0, True), at.c)
    own_x = pltpu.make_async_copy(xown, xall.at[at.g], lsem.at[4])
    own_x.start()
    z_up = zpost.send(xown, xall.at[at.g], up)
    z_down = zpost.send(xown, xall.at[at.g], down)
    z_over = [zpost.send(xown, xall.at[at.g], over)]
    def lay_q(j, _):
        for u in range(4):
            qbuf[pl.ds(pl.multiple_of(j * 128 + u * 32, 32), 32), :] = xa[pl.ds(4 * j + u, 32, stride=128), :].astype(BF16)
        return 0

    lax.fori_loop(0, IHEADS // 4, lay_q, 0)
    wt[...] = jnp.concatenate([xa[pl.ds(121, 32, stride=128), :], jnp.zeros((96, 128), F32)], axis=0).T
    wq[...] = jnp.concatenate([wt[pl.ds(u, 16, stride=4), 0:32] for u in range(4)], axis=1)
    select_rows(2)
    next(big)
    load_keys.wait()

    def index_block(b, _):
        k = keybuf[pl.ds(pl.multiple_of(b * KEYB, KEYB), KEYB), :]
        a = None
        for i in range(8):
            p = lax.dot_general(
                k, qbuf[i * 256 : i * 256 + 256, :], (((1,), (1,)), ((), ())), preferred_element_type=F32
            )
            for u in (0, 1):
                t = jnp.maximum(p[:, u * 128 : u * 128 + 128], 0.0) * wq[2 * i + u : 2 * i + u + 1, :]
                a = t if a is None else a + t
        a = a + pltpu.roll(a, 64, 1)
        a = (a + pltpu.roll(a, 32, 1)).T
        n = KEYB // 128
        scale = kscale[pl.ds(pl.multiple_of(b * n, n), n), :]
        for j in range(n):
            cols = pl.ds(pl.multiple_of(b * KEYB + j * 128, 128), 128)
            scores[:, cols] = a[0:32, j * 128 : j * 128 + 128] * scale[j : j + 1, :]
        return 0

    def index(b):
        lax.fori_loop(b, b + 1, index_block, 0)

    index(0)
    next(big)
    index(1)
    z_up.wait_recv()
    low = xall.at[at.grp(-1)]
    z_low = zpost.send(low.at[pl.ds(0, 16)], low.at[pl.ds(0, 16)], up)
    z_over.append(zpost.send(low, low, over))
    z_down.wait_recv()
    high_x = xall.at[at.grp(1)]
    z_high = zpost.send(high_x.at[pl.ds(16, 16)], high_x.at[pl.ds(16, 16)], down)
    z_over.append(zpost.send(high_x, high_x, over))
    next(big)
    index(2)
    next(big)
    select_rows(3)
    z_low.wait_recv()
    z_high.wait_recv()
    far = xall.at[at.grp(2)]
    z_over.append(zpost.send(far, far, over))
    index(3)
    for _ in big:
        pass
    for cp in z_over:
        cp.wait_recv()
    for cp in keeps + [own_x, keep_pos, own_q]:
        cp.wait()
    for post in (few, many, zpost):
        post.finish()


def gather_all(*args):
    dma = pltpu.SemaphoreType.DMA
    return pl.pallas_call(
        gather_kernel,
        out_shape=(
            jax.ShapeDtypeStruct((16, 2, WIDTH, HEADS), BF16),
            jax.ShapeDtypeStruct((16, 8, 128), jnp.int32),
            jax.ShapeDtypeStruct((8, 32, TOKW), BF16),
            jax.ShapeDtypeStruct((32, CAP, WIDTH), BF16),
            jax.ShapeDtypeStruct((32, CACHE), F32),
        ),
        in_specs=[pl.BlockSpec(memory_space=VMEM)] * 9 + [pl.BlockSpec(memory_space=ANY)] * 2,
        out_specs=(pl.BlockSpec(memory_space=ANY),) * 4 + (pl.BlockSpec(memory_space=VMEM),),
        scratch_shapes=[
            VMEM((256, 128), F32),
            VMEM((16, 8, 128), jnp.int32),
            VMEM((16, 2, 128, 128), BF16),
            VMEM((CACHE, IDIM), BF16),
            VMEM((32 * 128, 128), F32),
            VMEM((32, TOKW), BF16),
            VMEM((IHEADS * 32, 128), BF16),
            VMEM((128, 128), F32),
            VMEM((16, 128), F32),
            VMEM((WIDTH, CACHE), BF16),
            VMEM((CACHE * PITCH + 8, 128), F32),
            VMEM((CAP * PITCH + 8, 128), F32),
            VMEM((32, CAP, WIDTH), BF16),
            VMEM((16, 8, 128), jnp.int32),
            SMEM((16, 8, 128), jnp.int32),
            dma((8,)),
            dma((4,)),
            dma((5,)),
            dma((40,)),
            dma((40,)),
            dma((55,)),
            dma((55,)),
            dma((8,)),
            dma((8,)),
        ],
        compiler_params=pltpu.CompilerParams(collective_id=0, has_side_effects=True, vmem_limit_bytes=58 * 2**20),
    )(*args)


def merge(parts, lo, n):
    top = parts[0][1]
    for _, l in parts[1:]:
        top = jnp.maximum(top, l)
    es = [jnp.exp(l - top) for _, l in parts]
    tot = es[0]
    for e in es[1:]:
        tot = tot + e
    inv = 1.0 / tot
    diag = lax.broadcasted_iota(jnp.int32, (n, HEADS), 0) + lo == lax.broadcasted_iota(jnp.int32, (n, HEADS), 1)
    out = None
    for (o, _), e in zip(parts, es):
        w = jnp.broadcast_to((e * inv)[0:1], (n, HEADS))
        col = jnp.sum(jnp.where(diag, w, 0.0), axis=1, keepdims=True)
        term = o.astype(F32) * col
        out = term if out is None else out + term
    return out.astype(BF16), top + jnp.log(tot)


def attend_rows(at, counts, kbuf, qbuf, o, l, h, d):
    ids = [at.ctx(1 - h, d, e) for e in range(4)]
    ss = [jnp.dot(kbuf[2 * i + h], qbuf[i, h], preferred_element_type=F32) * SCALE for i in ids]
    ps = []
    for i, s in zip(ids, ss):
        live = lax.broadcasted_iota(jnp.int32, (CAP, HEADS), 0) < counts[i, 4, h]
        s = jnp.where(live, s, -1e30)
        m = jnp.max(s, axis=0, keepdims=True)
        e = jnp.where(live, jnp.exp(s - m), 0.0)
        n = jnp.sum(e, axis=0, keepdims=True)
        l[i, h] = jnp.broadcast_to(m + jnp.log(n), (8, HEADS))
        ps.append((e * (1.0 / n)).astype(BF16))
    for i, p in zip(ids, ps):
        v = kbuf[2 * i + h, :, 0:LATENT]
        o[i, h] = lax.dot_general(p, v, (((0,), (0,)), ((), ())), preferred_element_type=F32).astype(BF16)


def plane_scatter(post, at, work, o, l, bufs, result):
    r1, l1, m1, ml1, r2, l2, p1, pl1, r3, l3, m2, ml2, r4, l4 = bufs

    def both(src, lsrc, dst, ldst, dev):
        return post.send(src, dst, dev), post.send(lsrc, ldst, dev)

    def arrive(pair):
        for cp in pair:
            cp.wait_recv()

    s1, s2 = {}, {}
    for h in (0, 1):
        a = 1 - h
        work(h, 2)
        for e in range(4):
            i = at.ctx(a, 2, e)
            s1[h, e] = both(o.at[i, h], l.at[i, h], r1.at[h, e], l1.at[h, e], at.near(a, 1 if e < 2 else -1))
    yield
    for h in (0, 1):
        a = 1 - h
        work(h, 1)
        work(h, -1)
        for e in range(4):
            d = 0 if e >= 2 else 1
            i = at.ctx(a, 1 - 2 * d, e)
            s2[h, d, e] = both(o.at[i, h], l.at[i, h], r2.at[h, d, e], l2.at[h, d, e], at.near(a, 1 - 2 * d))
    yield
    for e in (0, 2, 1, 3):
        for h in (0, 1):
            a = 1 - h
            d = 0 if e < 2 else 1
            i = at.ctx(a, 1 - 2 * d, e)
            arrive(s1[h, e])
            m1[h, e], ml1[h, e] = merge([(o[i, h], l[i, h]), (r1[h, e], l1[h, e])], 0, HEADS)
            s2[h, d, e] = both(m1.at[h, e], ml1.at[h, e], r2.at[h, d, e], l2.at[h, d, e], at.near(a, 1 - 2 * d))
        if e == 2:
            yield
    work(0, 0)
    work(1, 0)
    yield
    s3, s4 = {}, {}
    for e in (2, 1, 3, 0):
        for h in (0, 1):
            a = 1 - h
            i = at.ctx(a, 0, e)
            arrive(s2[h, 0, e])
            arrive(s2[h, 1, e])
            p1[h, e], pl1[h, e] = merge(
                [(o[i, h], l[i, h]), (r2[h, 0, e], l2[h, 0, e]), (r2[h, 1, e], l2[h, 1, e])], 0, HEADS
            )
            if e == 2:
                for d in (0, 1):
                    s3[h, d] = both(
                        p1.at[h, 2, pl.ds(64 * d, 64)], pl1.at[h, 2], r3.at[h, d], l3.at[h, d], at.near(h, 1 - 2 * d)
                    )
        yield
    for h in (0, 1):
        for d in (0, 1):
            e = 1 if d == 0 else 3
            arrive(s3[h, d])
            mine = slice(64 * d, 64 * d + 64)
            rest = slice(64 - 64 * d, 128 - 64 * d)
            m2[h, d, rest] = p1[h, e, rest]
            m2[h, d, mine], lm = merge([(p1[h, e, mine], pl1[h, e]), (r3[h, d], l3[h, d])], 64 * d, 64)
            lane = lax.broadcasted_iota(jnp.int32, (8, HEADS), 1)
            ml2[h, d] = jnp.where((lane < 64) if d == 0 else (lane >= 64), lm, pl1[h, e])
            s4[h, d] = both(m2.at[h, d], ml2.at[h, d], r4.at[h, d], l4.at[h, d], at.near(h, 1 - 2 * d))
    yield
    for h in (0, 1):
        arrive(s4[h, 0])
        arrive(s4[h, 1])
        result[h], _ = merge([(p1[h, 0], pl1[h, 0]), (r4[h, 0], l4[h, 0]), (r4[h, 1], l4[h, 1])], 0, HEADS)


def reduce_kernel(
    counts, kg, qall, xall, gate, up, dn,
    attn, moe,
    kbuf, qbuf, o, l, tot,
    xbuf, wgu, dnbuf, acc, hid, mp, rc, rz1, rz2, yf, yb, ry,
    r1, l1, m1, ml1, r2, l2, p1, pl1, r3, l3, m2, ml2, r4, l4,
    rsem, lsem, ss, rs, zss, zrs,
):
    at = Place()
    near = {}
    def fetch(dx, dy):
        i = at.ctx(0, dx, dy)
        n = len(near)
        pair = pl.ds(2 * i, 2)
        near[dx, dy] = [
            pltpu.make_async_copy(kg.at[pair], kbuf.at[pair], rsem.at[2 * n]),
            pltpu.make_async_copy(qall.at[i], qbuf.at[i], rsem.at[2 * n + 1]),
        ]
        for cp in near[dx, dy]:
            cp.start()

    for dx, dy in [(2, 2), (0, 2), (1, 2), (3, 2), (2, 0), (2, 1), (2, 3)]:
        fetch(dx, dy)

    def work(h, d):
        for e in range(4):
            for cp in near.pop((e, d % 4) if h == 0 else (d % 4, e), ()):
                cp.wait()
        attend_rows(at, counts, kbuf, qbuf, o, l, h, d)

    loads = [pltpu.make_async_copy(xall, xbuf, lsem.at[0])]
    for e in (0, 1):
        loads.append(pltpu.make_async_copy(gate.at[e], wgu.at[e, :, pl.ds(0, 128)], lsem.at[1 + e]))
        loads.append(pltpu.make_async_copy(up.at[e], wgu.at[e, :, pl.ds(128, 128)], lsem.at[3 + e]))
    load_dn = pltpu.make_async_copy(dn, dnbuf, lsem.at[5])
    for cp in loads + [load_dn]:
        cp.start()
    for dx, dy in [(dx, dy) for dx in (1, 3, 0) for dy in (1, 3, 0)]:
        fetch(dx, dy)
    at.greet()
    post = Post(ss, rs)
    flow = plane_scatter(post, at, work, o, l, (r1, l1, m1, ml1, r2, l2, p1, pl1, r3, l3, m2, ml2, r4, l4), attn)
    next(flow)

    for cp in loads:
        cp.wait()
    acc[...] = jnp.zeros_like(acc)

    def expand(k, _):
        cols = pl.ds(pl.multiple_of(k * 1024, 1024), 1024)
        x = xbuf[:, :, cols].reshape(256, 1024)
        for e in (0, 1):
            acc[e] += jnp.dot(x, wgu[e, cols, :], preferred_element_type=F32)
        return 0

    lax.fori_loop(0, MODEL // 1024, expand, 0)
    gates = xbuf[:, :, MODEL:TOKW].reshape(256, 128).astype(F32)
    lane = lax.broadcasted_iota(jnp.int32, (256, 128), 1)
    for e in (0, 1):
        own = at.g * 2 + e
        col = jnp.sum(jnp.where((lane == own) | (lane == own + 16), gates, 0.0), axis=1, keepdims=True)
        gp, upart = acc[e, :, 0:128], acc[e, :, 128:256]
        hid[:, e * 128 : e * 128 + 128] = (gp / (1.0 + jnp.exp(-gp)) * upart * col).astype(BF16)
    load_dn.wait()

    def contract(k, _):
        cols = pl.ds(pl.multiple_of(k * 1024, 1024), 1024)
        mp[:, :, cols] = jnp.dot(hid[...], dnbuf[:, cols], preferred_element_type=F32).astype(BF16).reshape(8, 32, 1024)
        return 0

    lax.fori_loop(0, MODEL // 1024, contract, 0)
    zpost = Post(zss, zrs)
    zup, zdown, over = (at.grp(1), at.c), (at.grp(-1), at.c), (at.grp(0, True), at.c)
    order = (2, 1, -1, 0)
    swaps = [zpost.send(mp.at[at.grp(d, True)], rc.at[i], over) for i, d in enumerate(order)]
    next(flow)

    def add(i, d):
        swaps[i].wait_recv()
        b = at.grp(d)
        mp[b] = (mp[b].astype(F32) + rc[i].astype(F32)).astype(BF16)
        return mp.at[b]

    low, top = pl.ds(0, 16), pl.ds(16, 16)
    far = add(0, 2)
    za = zpost.send(far.at[low], rz1.at[0], zup)
    zb = zpost.send(far.at[top], rz1.at[1], zdown)
    above = add(1, 1)
    zc = [zpost.send(above.at[top], rz2.at[0, top], zup)]
    below = add(2, -1)
    zd = [zpost.send(below.at[low], rz2.at[1, low], zdown)]
    next(flow)
    next(flow)
    za.wait_recv()
    above[0:16] = (above[0:16].astype(F32) + rz1[0].astype(F32)).astype(BF16)
    zc.append(zpost.send(above.at[low], rz2.at[0, low], zup))
    zb.wait_recv()
    below[16:32] = (below[16:32].astype(F32) + rz1[1].astype(F32)).astype(BF16)
    zd.append(zpost.send(below.at[top], rz2.at[1, top], zdown))
    swaps[3].wait_recv()
    for _ in range(5):
        next(flow)
    for cp in zc + zd:
        cp.wait_recv()

    def spread(k, _):
        cols = pl.ds(pl.multiple_of(k * 128, 128), 128)
        t = mp[at.g, :, cols].astype(F32) + rc[3, :, cols].astype(F32)
        t = t + rz2[0, :, cols].astype(F32) + rz2[1, :, cols].astype(F32)
        yf[pl.ds(k, 32, stride=CHUNKS), :] = t
        return 0

    lax.fori_loop(0, CHUNKS, spread, 0)

    def narrow(i, _):
        yb[i] = yf[pl.ds(pl.multiple_of(i * 112, 8), 112), :].astype(BF16)
        return 0

    lax.fori_loop(0, 16, narrow, 0)
    home = [zpost.send(yb.at[at.peer(k)[1]], ry.at[k - 1], at.peer(k)) for k in range(1, 16)]
    for _ in flow:
        pass
    total = yb[at.c].astype(F32)
    for k, cp in enumerate(home):
        cp.wait_recv()
        total = total + ry[k].astype(F32)
    tot[...] = total
    for k in range(CHUNKS):
        moe[:, 128 * k : 128 * k + 128] = tot[pl.ds(k, 2, stride=CHUNKS), :].astype(BF16)
    post.finish()
    zpost.finish()


def reduce_all(*args):
    dma = pltpu.SemaphoreType.DMA
    ob, lb = (HEADS, LATENT), (8, HEADS)

    def pair(*lead, block=ob):
        return [VMEM(lead + block, BF16), VMEM(lead + lb, F32)]

    return pl.pallas_call(
        reduce_kernel,
        out_shape=(jax.ShapeDtypeStruct((2, HEADS, LATENT), BF16), jax.ShapeDtypeStruct((2, MODEL), BF16)),
        in_specs=[pl.BlockSpec(memory_space=SMEM)] + [pl.BlockSpec(memory_space=ANY)] * 6,
        out_specs=(pl.BlockSpec(memory_space=VMEM),) * 2,
        scratch_shapes=[
            VMEM((32, CAP, WIDTH), BF16),
            VMEM((16, 2, WIDTH, HEADS), BF16),
            VMEM((16, 2) + ob, BF16),
            VMEM((16, 2) + lb, F32),
            VMEM((112, 128), F32),
            VMEM((8, 32, TOKW), BF16),
            VMEM((2, MODEL, 256), BF16),
            VMEM((256, MODEL), BF16),
            VMEM((2, 256, 256), F32),
            VMEM((256, 256), BF16),
            VMEM((8, 32, MODEL), BF16),
            VMEM((4, 32, MODEL), BF16),
            VMEM((2, 16, MODEL), BF16),
            VMEM((2, 32, MODEL), BF16),
            VMEM((32 * CHUNKS, 128), F32),
            VMEM((16, 112, 128), BF16),
            VMEM((15, 112, 128), BF16),
            *pair(2, 4),
            *pair(2, 4),
            *pair(2, 2, 4),
            *pair(2, 4),
            *pair(2, 2, block=(64, LATENT)),
            *pair(2, 2),
            *pair(2, 2),
            dma((32,)),
            dma((6,)),
            dma((64,)),
            dma((64,)),
            dma((25,)),
            dma((25,)),
        ],
        compiler_params=pltpu.CompilerParams(collective_id=1, has_side_effects=True, vmem_limit_bytes=58 * 2**20),
    )(*args)


def local(
    index_query, index_weights, index_keys, key_scales, attn_query, compact_cache, top_pos, owner_counts,
    moe_input, expert_ids, expert_gates, gate_proj, up_proj, down_proj,
):
    qall, pall, xall, kg, index_scores = gather_all(
        index_query, index_weights, moe_input, expert_ids, expert_gates, top_pos, owner_counts,
        key_scales.reshape(CACHE // 128, 128), jnp.swapaxes(attn_query, 1, 2), index_keys, compact_cache.T,
    )
    attn_out, moe_out = reduce_all(
        pall, kg, qall, xall, gate_proj, up_proj, down_proj.reshape(256, MODEL)
    )
    return index_scores, attn_out, moe_out


def solution(mesh):
    one = P(("grp", "ctx"))
    in_specs = (one,) * 11 + (P("grp", None, "ctx"), P("grp", None, "ctx"), P("grp", "ctx", None))
    return jax.shard_map(
        local, mesh=mesh, in_specs=in_specs, out_specs=(P("grp", "ctx"), one, one), check_vma=False
    )
```

```python
import jax
import jax.numpy as jnp
from jax import lax
from jax.experimental import pallas as pl
from jax.experimental.pallas import tpu as pltpu
from jax.sharding import PartitionSpec as P

MESH = pl.DeviceIdType.MESH
BF16, F32 = jnp.bfloat16, jnp.float32
HEADS, LATENT, WIDTH = 128, 512, 576
IHEADS, IDIM = 64, 128
CACHE, CAP = 8192, 256
MODEL = 7168
CHUNKS = MODEL // 128
TOKW = MODEL + 128
HALF = 288
KEYB = 2048
PITCH = 5
SCALE = 192.0**-0.5
ANY, VMEM, SMEM = pl.ANY, pltpu.VMEM, pltpu.SMEM


class Place:
    def __init__(self):
        self.g, self.c = lax.axis_index("grp"), lax.axis_index("ctx")
        self.z, self.core = self.g // 2, lax.rem(self.g, 2)
        self.x, self.y = self.c // 4, lax.rem(self.c, 4)

    def ctx(self, axis, d, e=0):
        dx, dy = (d, e) if axis == 0 else (e, d)
        return lax.rem(self.x + dx + 4, 4) * 4 + lax.rem(self.y + dy + 4, 4)

    def near(self, axis, d):
        return (self.g, self.ctx(axis, d))

    def peer(self, k):
        return (self.g, lax.rem(self.c + k, 16))

    def grp(self, d, other=False):
        core = 1 - self.core if other else self.core
        return lax.rem(self.z + d + 4, 4) * 2 + core

    def greet(self):
        bar = pltpu.get_barrier_semaphore()
        friends = [self.peer(k) for k in range(1, 16)]
        friends += [(self.grp(1), self.c), (self.grp(-1), self.c), (self.grp(0, True), self.c)]
        for f in friends:
            pl.semaphore_signal(bar, inc=1, device_id=f, device_id_type=MESH)
        pl.semaphore_wait(bar, len(friends))


class Post:
    def __init__(self, send_sems, recv_sems):
        self.ss, self.rs, self.out = send_sems, recv_sems, []

    def send(self, src, dst, dev):
        i = len(self.out)
        cp = pltpu.make_async_remote_copy(
            src_ref=src, dst_ref=dst, send_sem=self.ss.at[i], recv_sem=self.rs.at[i], device_id=dev, device_id_type=MESH
        )
        cp.start()
        self.out.append(cp)
        return cp

    def finish(self):
        for cp in self.out:
            cp.wait_send()


def plane_gather(post, at, own, part):
    def both(ref, axis, src=None):
        src = ref if src is None else src
        return post.send(src, ref, at.near(axis, 1)), post.send(src, ref, at.near(axis, -1))

    def split(src, h, axis, plus, minus):
        plus.wait_recv()
        lo = part(src(-1), h, 0)
        a = post.send(lo, lo, at.near(axis, 1))
        minus.wait_recv()
        hi = part(src(1), h, 1)
        return a, post.send(hi, hi, at.near(axis, -1))

    first = [both(part(at.c, h, None), h, own.at[h]) for h in (0, 1)]
    across = {(h, 0): both(part(at.c, h, None), 1 - h, own.at[h]) for h in (0, 1)}
    yield
    second = []
    for h in (0, 1):
        second.append(split(lambda d: at.ctx(h, d), h, h, *first[h]))
        for d in (-1, 1):
            across[h, d] = both(part(at.ctx(h, d), h, None), 1 - h)
    yield
    for h in (0, 1):
        for cp in second[h]:
            cp.wait_recv()
        across[h, 2] = both(part(at.ctx(h, 2), h, None), 1 - h)
    last = []
    for d in (0, -1, 1, 2):
        yield
        for h in (0, 1):
            last += split(lambda e: at.ctx(h, d, e), h, 1 - h, *across[h, d])
    yield
    for cp in last:
        cp.wait_recv()


def gather_kernel(
    iq, iw, tok, ids, eg, tp, oc, kscale, aq, keys, cache,
    qall, pall, xall, kg, scores,
    stage, pst, agbuf, keybuf, xa, xown, qbuf, wt, wq, cbuf, rows, dst, kbf, posv, poss,
    csem, ksem, lsem, ss, rs, kss, krs, zss, zrs,
):
    at = Place()
    loads = []
    for i in range(8):
        cols = pl.ds(1024 * i, 1024)
        loads.append(pltpu.make_async_copy(cache.at[:, cols], cbuf.at[:, cols], csem.at[i]))
        loads[-1].start()
    own_q = pltpu.make_async_copy(aq, qall.at[at.c], lsem.at[1])
    own_q.start()
    load_keys = pltpu.make_async_copy(keys, keybuf, lsem.at[3])
    load_keys.start()

    stage[...] = jnp.zeros_like(stage)
    for j in range(IHEADS):
        stage[pl.ds(j, 2, stride=128), :] = iq[:, 128 * j : 128 * j + 128].astype(F32)
    for k in range(CHUNKS):
        stage[pl.ds(64 + k, 2, stride=128), :] = tok[:, 128 * k : 128 * k + 128].astype(F32)
    lane = lax.broadcasted_iota(jnp.int32, (2, 128), 1)
    table = jnp.zeros((2, 128), F32)
    for k in range(8):
        mine = (lane == ids[:, k : k + 1]) | (lane == ids[:, k : k + 1] + 16)
        table = table + jnp.where(mine, eg[:, k : k + 1], 0.0)
    high = table.astype(BF16).astype(F32)
    stage[pl.ds(120, 2, stride=128), :] = jnp.where(lane < 16, high, table - high)
    stage[pl.ds(121, 2, stride=128), 0:IHEADS] = iw[...].astype(F32)
    agbuf[at.c] = stage[...].reshape(2, 128, 128).astype(BF16)
    first_lane = lax.broadcasted_iota(jnp.int32, (1, 128), 1)
    for o in range(16):
        for h in (0, 1):
            for k in (0, 1):
                pst[o, 2 * h + k : 2 * h + k + 1, :] = tp[h, o : o + 1, 128 * k : 128 * k + 128] * PITCH
        pst[o, 4:5, :] = jnp.where(first_lane == 0, oc[0:1, o : o + 1], oc[1:2, o : o + 1])
        pst[o, 5:8, :] = jnp.zeros((3, 128), jnp.int32)
    at.greet()
    few = Post(kss, krs)
    quick = plane_gather(
        few, at, agbuf.at[at.c], lambda i, h, q: agbuf.at[i, h] if q is None else agbuf.at[i, h, pl.ds(64 * q, 64)]
    )
    next(quick)
    places = [few.send(pst.at[at.peer(k)[1]], posv.at[at.c], at.peer(k)) for k in range(1, 16)]
    own_pos = pltpu.make_async_copy(pst.at[at.c], posv.at[at.c], lsem.at[2])
    own_pos.start()
    many = Post(ss, rs)
    big = plane_gather(
        many, at, aq, lambda i, h, q: qall.at[i, h] if q is None else qall.at[i, h, pl.ds(HALF * q, HALF)]
    )
    next(big)

    eye = (
        lax.broadcasted_iota(jnp.int32, (256, 256), 0) == lax.broadcasted_iota(jnp.int32, (256, 256), 1)
    ).astype(BF16)

    def turn_rows(i):
        loads[i].wait()

        for b in range(4):
            off = i * 1024 + b * 256
            x = cbuf[:, off : off + 256]
            if b < 3:
                t = x.T.astype(F32)
            else:
                t = lax.dot_general(eye, x, (((1,), (1,)), ((), ())), preferred_element_type=F32)
            for c in range(5):
                w = min(128, WIDTH - 128 * c)
                rows[pl.ds(off * PITCH + c, 256, stride=PITCH), 0:w] = t[:, c * 128 : c * 128 + w]

    def select(t, _):
        c, line = t // 2, lax.rem(t, 2) * 2
        for u in range(CAP):
            p = poss[c, line + u // 128, u % 128]
            dst[pl.ds(u * PITCH, 8), :] = rows[pl.ds(p, 8), :]
        for i in range(5):
            n = min(128, WIDTH - 128 * i)
            kbf[t, :, i * 128 : i * 128 + n] = dst[pl.ds(i, CAP, stride=PITCH), 0:n].astype(BF16)
        return 0

    keeps = []

    def select_rows(i):
        lax.fori_loop(8 * i, 8 * i + 8, select, 0)
        part = pl.ds(8 * i, 8)
        keeps.append(pltpu.make_async_copy(kbf.at[part], kg.at[part], ksem.at[i]))
        keeps[-1].start()

    for i in range(4):
        turn_rows(i)
    next(quick)
    for i in range(4, 8):
        turn_rows(i)
    for cp in places:
        cp.wait_recv()
    own_pos.wait()
    to_smem = pltpu.make_async_copy(posv, poss, lsem.at[0])
    to_smem.start()
    keep_pos = pltpu.make_async_copy(posv, pall, lsem.at[2])
    keep_pos.start()
    next(quick)
    next(big)
    to_smem.wait()
    next(quick)
    select_rows(0)
    next(quick)
    next(quick)
    next(quick)
    for _ in quick:
        pass

    def widen(i, _):
        xa[pl.ds(pl.multiple_of(i * 256, 256), 256), :] = agbuf[i].reshape(256, 128).astype(F32)
        return 0

    lax.fori_loop(0, 16, widen, 0)

    def lay(k, _):
        for u in range(3):
            cols = pl.ds(pl.multiple_of(k * 384 + u * 128, 128), 128)
            xown[:, cols] = xa[pl.ds(64 + 3 * k + u, 32, stride=128), :].astype(BF16)
        return 0

    lax.fori_loop(0, (CHUNKS + 1) // 3, lay, 0)
    zpost = Post(zss, zrs)
    up, down, over = (at.grp(1), at.c), (at.grp(-1), at.c), (at.grp(0, True), at.c)
    own_x = pltpu.make_async_copy(xown, xall.at[at.g], lsem.at[4])
    own_x.start()
    z_up = zpost.send(xown, xall.at[at.g], up)
    z_down = zpost.send(xown, xall.at[at.g], down)
    z_over = [zpost.send(xown, xall.at[at.g], over)]
    def lay_q(j, _):
        for u in range(4):
            qbuf[pl.ds(pl.multiple_of(j * 128 + u * 32, 32), 32), :] = xa[pl.ds(4 * j + u, 32, stride=128), :].astype(BF16)
        return 0

    lax.fori_loop(0, IHEADS // 4, lay_q, 0)
    wt[...] = jnp.concatenate([xa[pl.ds(121, 32, stride=128), :], jnp.zeros((96, 128), F32)], axis=0).T
    wq[...] = jnp.concatenate([wt[pl.ds(u, 16, stride=4), 0:32] for u in range(4)], axis=1)
    next(big)
    select_rows(1)
    select_rows(2)
    next(big)
    load_keys.wait()

    def index_block(b, _):
        k = keybuf[pl.ds(pl.multiple_of(b * KEYB, KEYB), KEYB), :]
        a = None
        for i in range(8):
            p = lax.dot_general(
                k, qbuf[i * 256 : i * 256 + 256, :], (((1,), (1,)), ((), ())), preferred_element_type=F32
            )
            for u in (0, 1):
                t = jnp.maximum(p[:, u * 128 : u * 128 + 128], 0.0) * wq[2 * i + u : 2 * i + u + 1, :]
                a = t if a is None else a + t
        a = a + pltpu.roll(a, 64, 1)
        a = (a + pltpu.roll(a, 32, 1)).T
        n = KEYB // 128
        scale = kscale[pl.ds(pl.multiple_of(b * n, n), n), :]
        for j in range(n):
            cols = pl.ds(pl.multiple_of(b * KEYB + j * 128, 128), 128)
            scores[:, cols] = a[0:32, j * 128 : j * 128 + 128] * scale[j : j + 1, :]
        return 0

    def index(b):
        lax.fori_loop(b, b + 1, index_block, 0)

    index(0)
    next(big)
    index(1)
    z_up.wait_recv()
    low = xall.at[at.grp(-1)]
    z_low = zpost.send(low.at[pl.ds(0, 16)], low.at[pl.ds(0, 16)], up)
    z_over.append(zpost.send(low, low, over))
    z_down.wait_recv()
    high_x = xall.at[at.grp(1)]
    z_high = zpost.send(high_x.at[pl.ds(16, 16)], high_x.at[pl.ds(16, 16)], down)
    z_over.append(zpost.send(high_x, high_x, over))
    next(big)
    index(2)
    next(big)
    select_rows(3)
    z_low.wait_recv()
    z_high.wait_recv()
    far = xall.at[at.grp(2)]
    z_over.append(zpost.send(far, far, over))
    index(3)
    for _ in big:
        pass
    for cp in z_over:
        cp.wait_recv()
    for cp in keeps + [own_x, keep_pos, own_q]:
        cp.wait()
    for post in (few, many, zpost):
        post.finish()


def gather_all(*args):
    dma = pltpu.SemaphoreType.DMA
    return pl.pallas_call(
        gather_kernel,
        out_shape=(
            jax.ShapeDtypeStruct((16, 2, WIDTH, HEADS), BF16),
            jax.ShapeDtypeStruct((16, 8, 128), jnp.int32),
            jax.ShapeDtypeStruct((8, 32, TOKW), BF16),
            jax.ShapeDtypeStruct((32, CAP, WIDTH), BF16),
            jax.ShapeDtypeStruct((32, CACHE), F32),
        ),
        in_specs=[pl.BlockSpec(memory_space=VMEM)] * 9 + [pl.BlockSpec(memory_space=ANY)] * 2,
        out_specs=(pl.BlockSpec(memory_space=ANY),) * 4 + (pl.BlockSpec(memory_space=VMEM),),
        scratch_shapes=[
            VMEM((256, 128), F32),
            VMEM((16, 8, 128), jnp.int32),
            VMEM((16, 2, 128, 128), BF16),
            VMEM((CACHE, IDIM), BF16),
            VMEM((32 * 128, 128), F32),
            VMEM((32, TOKW), BF16),
            VMEM((IHEADS * 32, 128), BF16),
            VMEM((128, 128), F32),
            VMEM((16, 128), F32),
            VMEM((WIDTH, CACHE), BF16),
            VMEM((CACHE * PITCH + 8, 128), F32),
            VMEM((CAP * PITCH + 8, 128), F32),
            VMEM((32, CAP, WIDTH), BF16),
            VMEM((16, 8, 128), jnp.int32),
            SMEM((16, 8, 128), jnp.int32),
            dma((8,)),
            dma((4,)),
            dma((5,)),
            dma((40,)),
            dma((40,)),
            dma((55,)),
            dma((55,)),
            dma((8,)),
            dma((8,)),
        ],
        compiler_params=pltpu.CompilerParams(collective_id=0, has_side_effects=True, vmem_limit_bytes=58 * 2**20),
    )(*args)


def merge(parts, lo, n):
    top = parts[0][1]
    for _, l in parts[1:]:
        top = jnp.maximum(top, l)
    es = [jnp.exp(l - top) for _, l in parts]
    tot = es[0]
    for e in es[1:]:
        tot = tot + e
    inv = 1.0 / tot
    diag = lax.broadcasted_iota(jnp.int32, (n, HEADS), 0) + lo == lax.broadcasted_iota(jnp.int32, (n, HEADS), 1)
    out = None
    for (o, _), e in zip(parts, es):
        w = jnp.broadcast_to((e * inv)[0:1], (n, HEADS))
        col = jnp.sum(jnp.where(diag, w, 0.0), axis=1, keepdims=True)
        term = o.astype(F32) * col
        out = term if out is None else out + term
    return out.astype(BF16), top + jnp.log(tot)


def attend_rows(at, counts, kbuf, qbuf, o, l, h, d):
    ids = [at.ctx(1 - h, d, e) for e in range(4)]
    ss = [jnp.dot(kbuf[2 * i + h], qbuf[i, h], preferred_element_type=F32) * SCALE for i in ids]
    ps = []
    for i, s in zip(ids, ss):
        live = lax.broadcasted_iota(jnp.int32, (CAP, HEADS), 0) < counts[i, 4, h]
        s = jnp.where(live, s, -1e30)
        m = jnp.max(s, axis=0, keepdims=True)
        e = jnp.where(live, jnp.exp(s - m), 0.0)
        n = jnp.sum(e, axis=0, keepdims=True)
        l[i, h] = jnp.broadcast_to(m + jnp.log(n), (8, HEADS))
        ps.append((e * (1.0 / n)).astype(BF16))
    for i, p in zip(ids, ps):
        v = kbuf[2 * i + h, :, 0:LATENT]
        o[i, h] = lax.dot_general(p, v, (((0,), (0,)), ((), ())), preferred_element_type=F32).astype(BF16)


def plane_scatter(post, at, work, o, l, bufs, result):
    r1, l1, m1, ml1, r2, l2, p1, pl1, r3, l3, m2, ml2, r4, l4 = bufs

    def both(src, lsrc, dst, ldst, dev):
        return post.send(src, dst, dev), post.send(lsrc, ldst, dev)

    def arrive(pair):
        for cp in pair:
            cp.wait_recv()

    s1, s2 = {}, {}
    for h in (0, 1):
        a = 1 - h
        work(h, 2)
        for e in range(4):
            i = at.ctx(a, 2, e)
            s1[h, e] = both(o.at[i, h], l.at[i, h], r1.at[h, e], l1.at[h, e], at.near(a, 1 if e < 2 else -1))
    yield
    for h in (0, 1):
        a = 1 - h
        work(h, 1)
        work(h, -1)
        for e in range(4):
            d = 0 if e >= 2 else 1
            i = at.ctx(a, 1 - 2 * d, e)
            s2[h, d, e] = both(o.at[i, h], l.at[i, h], r2.at[h, d, e], l2.at[h, d, e], at.near(a, 1 - 2 * d))
        yield
    for e in (0, 2, 1, 3):
        for h in (0, 1):
            a = 1 - h
            d = 0 if e < 2 else 1
            i = at.ctx(a, 1 - 2 * d, e)
            arrive(s1[h, e])
            m1[h, e], ml1[h, e] = merge([(o[i, h], l[i, h]), (r1[h, e], l1[h, e])], 0, HEADS)
            s2[h, d, e] = both(m1.at[h, e], ml1.at[h, e], r2.at[h, d, e], l2.at[h, d, e], at.near(a, 1 - 2 * d))
        if e == 2:
            yield
    work(0, 0)
    work(1, 0)
    yield
    s3, s4 = {}, {}
    for e in (2, 1, 3, 0):
        for h in (0, 1):
            a = 1 - h
            i = at.ctx(a, 0, e)
            arrive(s2[h, 0, e])
            arrive(s2[h, 1, e])
            p1[h, e], pl1[h, e] = merge(
                [(o[i, h], l[i, h]), (r2[h, 0, e], l2[h, 0, e]), (r2[h, 1, e], l2[h, 1, e])], 0, HEADS
            )
            if e == 2:
                for d in (0, 1):
                    s3[h, d] = both(
                        p1.at[h, 2, pl.ds(64 * d, 64)], pl1.at[h, 2], r3.at[h, d], l3.at[h, d], at.near(h, 1 - 2 * d)
                    )
        yield
    for h in (0, 1):
        for d in (0, 1):
            e = 1 if d == 0 else 3
            arrive(s3[h, d])
            mine = slice(64 * d, 64 * d + 64)
            rest = slice(64 - 64 * d, 128 - 64 * d)
            m2[h, d, rest] = p1[h, e, rest]
            m2[h, d, mine], lm = merge([(p1[h, e, mine], pl1[h, e]), (r3[h, d], l3[h, d])], 64 * d, 64)
            lane = lax.broadcasted_iota(jnp.int32, (8, HEADS), 1)
            ml2[h, d] = jnp.where((lane < 64) if d == 0 else (lane >= 64), lm, pl1[h, e])
            s4[h, d] = both(m2.at[h, d], ml2.at[h, d], r4.at[h, d], l4.at[h, d], at.near(h, 1 - 2 * d))
    yield
    for h in (0, 1):
        arrive(s4[h, 0])
        arrive(s4[h, 1])
        result[h], _ = merge([(p1[h, 0], pl1[h, 0]), (r4[h, 0], l4[h, 0]), (r4[h, 1], l4[h, 1])], 0, HEADS)


def reduce_kernel(
    counts, kg, qall, xall, gate, up, dn,
    attn, moe,
    kbuf, qbuf, o, l, tot,
    xbuf, wgu, dnbuf, acc, hid, mp, rc, rz1, rz2, yf, yb, ry,
    r1, l1, m1, ml1, r2, l2, p1, pl1, r3, l3, m2, ml2, r4, l4,
    rsem, lsem, ss, rs, zss, zrs,
):
    at = Place()
    near = {}
    def fetch(dx, dy):
        i = at.ctx(0, dx, dy)
        n = len(near)
        pair = pl.ds(2 * i, 2)
        near[dx, dy] = [
            pltpu.make_async_copy(kg.at[pair], kbuf.at[pair], rsem.at[2 * n]),
            pltpu.make_async_copy(qall.at[i], qbuf.at[i], rsem.at[2 * n + 1]),
        ]
        for cp in near[dx, dy]:
            cp.start()

    for dx, dy in [(2, 2), (0, 2), (1, 2), (3, 2), (2, 0), (2, 1), (2, 3)]:
        fetch(dx, dy)

    def work(h, d):
        for e in range(4):
            for cp in near.pop((e, d % 4) if h == 0 else (d % 4, e), ()):
                cp.wait()
        attend_rows(at, counts, kbuf, qbuf, o, l, h, d)

    loads = [pltpu.make_async_copy(xall, xbuf, lsem.at[0])]
    for e in (0, 1):
        loads.append(pltpu.make_async_copy(gate.at[e], wgu.at[e, :, pl.ds(0, 128)], lsem.at[1 + e]))
        loads.append(pltpu.make_async_copy(up.at[e], wgu.at[e, :, pl.ds(128, 128)], lsem.at[3 + e]))
    load_dn = pltpu.make_async_copy(dn, dnbuf, lsem.at[5])
    for cp in loads + [load_dn]:
        cp.start()
    for dx, dy in [(dx, dy) for dx in (1, 3, 0) for dy in (1, 3, 0)]:
        fetch(dx, dy)
    at.greet()
    post = Post(ss, rs)
    flow = plane_scatter(post, at, work, o, l, (r1, l1, m1, ml1, r2, l2, p1, pl1, r3, l3, m2, ml2, r4, l4), attn)
    next(flow)

    for cp in loads:
        cp.wait()
    acc[...] = jnp.zeros_like(acc)

    def expand(k, _):
        cols = pl.ds(pl.multiple_of(k * 1024, 1024), 1024)
        x = xbuf[:, :, cols].reshape(256, 1024)
        for e in (0, 1):
            acc[e] += jnp.dot(x, wgu[e, cols, :], preferred_element_type=F32)
        return 0

    lax.fori_loop(0, MODEL // 1024, expand, 0)
    gates = xbuf[:, :, MODEL:TOKW].reshape(256, 128).astype(F32)
    lane = lax.broadcasted_iota(jnp.int32, (256, 128), 1)
    for e in (0, 1):
        own = at.g * 2 + e
        col = jnp.sum(jnp.where((lane == own) | (lane == own + 16), gates, 0.0), axis=1, keepdims=True)
        gp, upart = acc[e, :, 0:128], acc[e, :, 128:256]
        hid[:, e * 128 : e * 128 + 128] = (gp / (1.0 + jnp.exp(-gp)) * upart * col).astype(BF16)
    load_dn.wait()

    def contract(k, _):
        cols = pl.ds(pl.multiple_of(k * 1024, 1024), 1024)
        mp[:, :, cols] = jnp.dot(hid[...], dnbuf[:, cols], preferred_element_type=F32).astype(BF16).reshape(8, 32, 1024)
        return 0

    lax.fori_loop(0, MODEL // 1024, contract, 0)
    zpost = Post(zss, zrs)
    zup, zdown, over = (at.grp(1), at.c), (at.grp(-1), at.c), (at.grp(0, True), at.c)
    order = (2, 1, -1, 0)
    swaps = [zpost.send(mp.at[at.grp(d, True)], rc.at[i], over) for i, d in enumerate(order)]
    next(flow)

    def add(i, d):
        swaps[i].wait_recv()
        b = at.grp(d)
        mp[b] = (mp[b].astype(F32) + rc[i].astype(F32)).astype(BF16)
        return mp.at[b]

    low, top = pl.ds(0, 16), pl.ds(16, 16)
    far = add(0, 2)
    za = zpost.send(far.at[low], rz1.at[0], zup)
    zb = zpost.send(far.at[top], rz1.at[1], zdown)
    next(flow)
    above = add(1, 1)
    zc = [zpost.send(above.at[top], rz2.at[0, top], zup)]
    below = add(2, -1)
    zd = [zpost.send(below.at[low], rz2.at[1, low], zdown)]
    next(flow)
    next(flow)
    za.wait_recv()
    above[0:16] = (above[0:16].astype(F32) + rz1[0].astype(F32)).astype(BF16)
    zc.append(zpost.send(above.at[low], rz2.at[0, low], zup))
    zb.wait_recv()
    below[16:32] = (below[16:32].astype(F32) + rz1[1].astype(F32)).astype(BF16)
    zd.append(zpost.send(below.at[top], rz2.at[1, top], zdown))
    swaps[3].wait_recv()
    for _ in range(5):
        next(flow)
    for cp in zc + zd:
        cp.wait_recv()

    def spread(k, _):
        cols = pl.ds(pl.multiple_of(k * 128, 128), 128)
        t = mp[at.g, :, cols].astype(F32) + rc[3, :, cols].astype(F32)
        t = t + rz2[0, :, cols].astype(F32) + rz2[1, :, cols].astype(F32)
        yf[pl.ds(k, 32, stride=CHUNKS), :] = t
        return 0

    lax.fori_loop(0, CHUNKS, spread, 0)

    def narrow(i, _):
        yb[i] = yf[pl.ds(pl.multiple_of(i * 112, 8), 112), :].astype(BF16)
        return 0

    lax.fori_loop(0, 16, narrow, 0)
    home = [zpost.send(yb.at[at.peer(k)[1]], ry.at[k - 1], at.peer(k)) for k in range(1, 16)]
    for _ in flow:
        pass
    total = yb[at.c].astype(F32)
    for k, cp in enumerate(home):
        cp.wait_recv()
        total = total + ry[k].astype(F32)
    tot[...] = total
    for k in range(CHUNKS):
        moe[:, 128 * k : 128 * k + 128] = tot[pl.ds(k, 2, stride=CHUNKS), :].astype(BF16)
    post.finish()
    zpost.finish()


def reduce_all(*args):
    dma = pltpu.SemaphoreType.DMA
    ob, lb = (HEADS, LATENT), (8, HEADS)

    def pair(*lead, block=ob):
        return [VMEM(lead + block, BF16), VMEM(lead + lb, F32)]

    return pl.pallas_call(
        reduce_kernel,
        out_shape=(jax.ShapeDtypeStruct((2, HEADS, LATENT), BF16), jax.ShapeDtypeStruct((2, MODEL), BF16)),
        in_specs=[pl.BlockSpec(memory_space=SMEM)] + [pl.BlockSpec(memory_space=ANY)] * 6,
        out_specs=(pl.BlockSpec(memory_space=VMEM),) * 2,
        scratch_shapes=[
            VMEM((32, CAP, WIDTH), BF16),
            VMEM((16, 2, WIDTH, HEADS), BF16),
            VMEM((16, 2) + ob, BF16),
            VMEM((16, 2) + lb, F32),
            VMEM((112, 128), F32),
            VMEM((8, 32, TOKW), BF16),
            VMEM((2, MODEL, 256), BF16),
            VMEM((256, MODEL), BF16),
            VMEM((2, 256, 256), F32),
            VMEM((256, 256), BF16),
            VMEM((8, 32, MODEL), BF16),
            VMEM((4, 32, MODEL), BF16),
            VMEM((2, 16, MODEL), BF16),
            VMEM((2, 32, MODEL), BF16),
            VMEM((32 * CHUNKS, 128), F32),
            VMEM((16, 112, 128), BF16),
            VMEM((15, 112, 128), BF16),
            *pair(2, 4),
            *pair(2, 4),
            *pair(2, 2, 4),
            *pair(2, 4),
            *pair(2, 2, block=(64, LATENT)),
            *pair(2, 2),
            *pair(2, 2),
            dma((32,)),
            dma((6,)),
            dma((64,)),
            dma((64,)),
            dma((25,)),
            dma((25,)),
        ],
        compiler_params=pltpu.CompilerParams(collective_id=1, has_side_effects=True, vmem_limit_bytes=58 * 2**20),
    )(*args)


def local(
    index_query, index_weights, index_keys, key_scales, attn_query, compact_cache, top_pos, owner_counts,
    moe_input, expert_ids, expert_gates, gate_proj, up_proj, down_proj,
):
    qall, pall, xall, kg, index_scores = gather_all(
        index_query, index_weights, moe_input, expert_ids, expert_gates, top_pos, owner_counts,
        key_scales.reshape(CACHE // 128, 128), jnp.swapaxes(attn_query, 1, 2), index_keys, compact_cache.T,
    )
    attn_out, moe_out = reduce_all(
        pall, kg, qall, xall, gate_proj, up_proj, down_proj.reshape(256, MODEL)
    )
    return index_scores, attn_out, moe_out


def solution(mesh):
    one = P(("grp", "ctx"))
    in_specs = (one,) * 11 + (P("grp", None, "ctx"), P("grp", None, "ctx"), P("grp", "ctx", None))
    return jax.shard_map(
        local, mesh=mesh, in_specs=in_specs, out_specs=(P("grp", "ctx"), one, one), check_vma=False
    )
```
